512 devices in a mesh: row: 8 (over x, core), col: 16 (over z_lo, y), layer: 4 (over z_hi).
Axes of the slice: x: 4, y: 4, z: 16 (z_hi: 4, z_lo: 4; z = z_hi * 4 + z_lo), core: 2. Of those that a mesh axis runs over, the one named last changes fastest.
Arguments:
- adjacency: bfloat16 [16, 512, 8192], P('col', 'row'), may hold values from 0 to 1.953125, as said below
- block_mask: int32 [64, 64], replicated, may hold values from 0 to 1, as said below
- prune_mask: int32 [64, 64], replicated, may hold values from 0 to 1, as said below
Outputs:
- expanded: float32 [16, 512, 8192], P(None, ('row', 'layer'), 'col')
The draws below stay inside these ranges and needn't reach their ends.
Inputs may be any that keep to these rules, and one draw needn't show every extreme that they name: `block_mask`: 1 marks a block of 128 x 128 adjacency entries that holds edges, 0 one that is dropped. `prune_mask`: 1 keeps a block of the expanded matrix, 0 prunes it; every diagonal block is kept. `adjacency`: entries are nonnegative.
All inputs are finite; a program needn't handle non-finite values.
Results may differ from the reference program's by a relative error of at most 0.015.
Values may be sent and summed in bfloat16 or wider, within the bound.
No kernel may reach another device: no remote copies, remote signals or barrier semaphores. Data moves between devices by JAX's collectives and lax.ppermute only.
A program may use at most 64 MiB of HBM per device.

```python
import math
import jax
import jax.numpy as jnp

RDEV = 64
BLK = 128
NODES = 8192
NBLK = 64
N_ROW = 8
N_COL = 16


def holder_index(node_ids):
    holder = node_ids // RDEV
    return holder % N_ROW * N_COL + holder // N_ROW


def draw_adjacency(key, part):
    key = jax.random.fold_in(key, 11)
    base_key, row_key, col_key = jax.random.split(key, 3)
    shape = (N_COL, NODES // N_COL, NODES)
    base = jnp.exp(jax.random.uniform(base_key, shape, jnp.float32, math.log(0.01), 0.0))
    row_scale = jnp.exp(jax.random.uniform(row_key, (N_COL, NODES // N_COL, 1), jnp.float32, 0.0, math.log(10.0)))
    col_scale = jnp.exp(jax.random.uniform(col_key, (1, 1, NODES), jnp.float32, 0.0, math.log(10.0)))
    factor = 8.0 / NODES
    node_ids = jnp.arange(NODES, dtype=jnp.int32)
    total = N_ROW * N_COL
    row_holder = holder_index(node_ids).reshape(N_COL, NODES // N_COL, 1)
    col_holder = holder_index(node_ids).reshape(1, 1, NODES)
    paired = (row_holder + total // 2) % total == col_holder
    boost = jnp.where(paired, 20.0, 1.0).astype(jnp.float32)
    return (base * row_scale * col_scale * boost * factor).astype(jnp.bfloat16)


def draw_block_mask(key, part):
    key = jax.random.fold_in(key, 5)
    density_key, picked_key = jax.random.split(key)
    density = jax.random.randint(density_key, (NBLK, 1), 1, 33)
    picked = jax.random.randint(picked_key, (NBLK, NBLK), 0, 64)
    return (picked < density).astype(jnp.int32)


def draw_prune_mask(key, part):
    key = jax.random.fold_in(key, 9)
    picked = jax.random.randint(key, (NBLK, NBLK), 0, 4)
    diagonal = jnp.arange(NBLK)[:, None] == jnp.arange(NBLK)[None, :]
    return ((picked > 0) | diagonal).astype(jnp.int32)


def setup_inputs(seed: int = 0) -> dict:
    splits = jax.random.split(jax.random.key(seed), 4)
    return {
        "adjacency": draw_adjacency(jax.random.fold_in(splits[3], 71), 0),
        "block_mask": draw_block_mask(jax.random.fold_in(splits[3], 71), 0),
        "prune_mask": draw_prune_mask(jax.random.fold_in(splits[3], 71), 0),
    }


def reference(adjacency, block_mask, prune_mask):
    node_count = adjacency.shape[2]
    adjacency_flat = adjacency.reshape(node_count, node_count)
    block_keep = jnp.repeat(jnp.repeat(block_mask, BLK, axis=0), BLK, axis=1)
    masked = adjacency_flat * block_keep.astype(jnp.bfloat16)
    identity = jnp.eye(node_count, dtype=jnp.float32)
    symmetric = (masked.astype(jnp.float32) + masked.T.astype(jnp.float32) + identity).astype(jnp.bfloat16)
    degree = jnp.sum(symmetric.astype(jnp.float32), axis=0)
    stochastic = (symmetric.astype(jnp.float32) / degree[None, :]).astype(jnp.bfloat16)
    product = jnp.dot(stochastic, stochastic, preferred_element_type=jnp.float32)
    prune_keep = jnp.repeat(jnp.repeat(prune_mask, BLK, axis=0), BLK, axis=1).astype(jnp.float32)
    inflated = product * product * prune_keep
    column_mass = jnp.sum(inflated, axis=0)
    expanded = node_count * inflated / column_mass[None, :]
    return expanded.reshape(N_COL, node_count // N_COL, node_count)
```

```python
import jax
import jax.numpy as jnp
from jax import lax
from jax.sharding import Mesh, PartitionSpec as P

BLK = 128


def on_device(adjacency, block_mask, prune_mask):
    bf16, f32 = jnp.bfloat16, jnp.float32
    rows_dev = adjacency.shape[1]
    node_count = adjacency.shape[2]
    nx, nk, nz, ny, nl = (lax.axis_size(a) for a in ("x", "core", "zlo", "y", "zhi"))
    nc = nz * ny
    x_id, k_id = lax.axis_index("x"), lax.axis_index("core")
    c_id = lax.axis_index("zlo") * ny + lax.axis_index("y")
    l_id = lax.axis_index("zhi")
    part = rows_dev // nl
    half = node_count // nk
    own_block = c_id * nx + x_id
    keep = lax.dynamic_slice_in_dim(block_mask, own_block, 1, 0)[0].astype(bf16)
    masked = adjacency[0].reshape(rows_dev, nc, nx, BLK) * keep.reshape(1, nc, nx, 1)
    outgoing = masked.transpose(2, 1, 0, 3).reshape(nx * nc, rows_dev, BLK)
    received = lax.all_to_all(outgoing, ("x", "zlo", "y"), split_axis=0, concat_axis=0, tiled=True)
    flipped = received.reshape(half, BLK).T
    halves = masked.reshape(rows_dev, nc, nx, nk, rows_dev).transpose(3, 0, 2, 1, 4)
    halves = halves.reshape(nk, rows_dev, half)
    kept = jnp.where(k_id == 0, halves[0], halves[1])
    given = jnp.where(k_id == 0, halves[1], halves[0])
    other = lax.ppermute(given, "core", [(0, 1), (1, 0)])
    direct = jnp.concatenate(
        [jnp.where(k_id == 0, kept, other), jnp.where(k_id == 0, other, kept)], axis=0
    )
    own_row = jnp.arange(nk * rows_dev, dtype=jnp.int32)
    own_col = (x_id * nc + c_id) * rows_dev + own_row - k_id * rows_dev
    col_ids = jnp.arange(half, dtype=jnp.int32)
    in_core = (own_row // rows_dev == k_id)[:, None]
    diagonal = ((own_col[:, None] == col_ids[None, :]) & in_core).astype(f32)
    block = (direct.astype(f32) + flipped.astype(f32) + diagonal).astype(bf16)
    block_rows = block.reshape(nk, nl, part, half)
    shard = lax.dynamic_slice_in_dim(block_rows, l_id, 1, 1).reshape(nk * part, half)
    left = lax.all_gather(shard, ("zlo", "y"), axis=0, tiled=True)
    blocks = [block] + [
        lax.ppermute(block, "x", [(i, (i + o) % nx) for i in range(nx)]) for o in range(1, nx)
    ]
    degree_chip = lax.psum(jnp.sum(block.astype(f32), axis=1), "core").reshape(nk, rows_dev)
    degree_own = jnp.where(k_id == 0, degree_chip[0], degree_chip[1])
    spread = jnp.broadcast_to(degree_own[None], (nx * nc, rows_dev))
    degree = lax.all_to_all(spread, ("x", "zlo", "y"), split_axis=0, concat_axis=0, tiled=True)
    scale = 1.0 / degree.reshape(1, half)
    order = (x_id - jnp.arange(nx)) % nx
    right = jnp.stack(blocks)[order].reshape(nx * BLK, half)
    right = (right.astype(f32) * scale).astype(bf16)
    partial = lax.dot_general(left, right, (((1,), (1,)), ((), ())), preferred_element_type=f32)
    partial = partial.reshape(nc, nk, part, nx * BLK)
    mine = jnp.where(k_id == 0, partial[:, 0], partial[:, 1])
    theirs = jnp.where(k_id == 0, partial[:, 1], partial[:, 0])
    summed = mine + lax.ppermute(theirs, "core", [(0, 1), (1, 0)])
    prune = prune_mask.reshape(nc, nx, nc, nx)
    prune = lax.dynamic_index_in_dim(prune, x_id, 1, keepdims=False)
    prune = lax.dynamic_index_in_dim(prune, c_id, 1, keepdims=False)
    prune = jnp.repeat(prune.astype(f32), BLK, axis=1)
    pruned = summed * summed * prune[:, None, :]
    mass = jnp.sum(pruned, axis=(0, 1))
    for axis in ("core", "x", "zhi"):
        mass = lax.psum(mass, axis)
    return pruned * (node_count / mass)[None, None, :]


def solution(mesh):
    rows, cols, layers = mesh.devices.shape
    devices = mesh.devices.reshape(rows // 2, 2, cols // 4, 4, layers)
    split = Mesh(devices, ("x", "core", "zlo", "y", "zhi"))
    in_specs = (P(("zlo", "y"), ("x", "core"), None), P(), P())
    out_specs = P(None, ("x", "core", "zhi"), ("zlo", "y"))
    return jax.shard_map(
        on_device, mesh=split, in_specs=in_specs, out_specs=out_specs, check_vma=False
    )
```

```python
import jax
import jax.numpy as jnp
from jax import lax
from jax.sharding import Mesh, PartitionSpec as P

BLK = 128


def on_device(adjacency, block_mask, prune_mask):
    bf16, f32 = jnp.bfloat16, jnp.float32
    rows_dev = adjacency.shape[1]
    node_count = adjacency.shape[2]
    nx, nk, nz, ny, nl = (lax.axis_size(a) for a in ("x", "core", "zlo", "y", "zhi"))
    nc = nz * ny
    x_id, k_id = lax.axis_index("x"), lax.axis_index("core")
    c_id = lax.axis_index("zlo") * ny + lax.axis_index("y")
    l_id = lax.axis_index("zhi")
    part = rows_dev // nl
    half = node_count // nk
    own_block = c_id * nx + x_id
    keep = lax.dynamic_slice_in_dim(block_mask, own_block, 1, 0)[0].astype(bf16)
    masked = adjacency[0].reshape(rows_dev, nc, nx, BLK) * keep.reshape(1, nc, nx, 1)
    outgoing = masked.transpose(2, 1, 0, 3).reshape(nx * nc, rows_dev, BLK)
    received = lax.all_to_all(outgoing, ("x", "zlo", "y"), split_axis=0, concat_axis=0, tiled=True)
    flipped = received.reshape(half, BLK).T
    halves = masked.reshape(rows_dev, nc, nx, nk, rows_dev).transpose(3, 0, 2, 1, 4)
    halves = halves.reshape(nk, rows_dev, half)
    kept = jnp.where(k_id == 0, halves[0], halves[1])
    given = jnp.where(k_id == 0, halves[1], halves[0])
    other = lax.ppermute(given, "core", [(0, 1), (1, 0)])
    direct = jnp.concatenate(
        [jnp.where(k_id == 0, kept, other), jnp.where(k_id == 0, other, kept)], axis=0
    )
    own_row = jnp.arange(nk * rows_dev, dtype=jnp.int32)
    own_col = (x_id * nc + c_id) * rows_dev + own_row - k_id * rows_dev
    col_ids = jnp.arange(half, dtype=jnp.int32)
    in_core = (own_row // rows_dev == k_id)[:, None]
    diagonal = ((own_col[:, None] == col_ids[None, :]) & in_core).astype(f32)
    block = (direct.astype(f32) + flipped.astype(f32) + diagonal).astype(bf16)
    block_rows = block.reshape(nk, nl, part, half)
    z_id = l_id * nz + lax.axis_index("zlo")

    def shard_for(step):
        layer = (z_id + step) % (nz * nl) // nz
        return lax.dynamic_slice_in_dim(block_rows, layer, 1, 1).reshape(nk * part, half)

    def z_pairs(step):
        spots = [(z, (z + step) % (nz * nl)) for z in range(nz * nl)]
        return [(a % nz * nl + a // nz, b % nz * nl + b // nz) for a, b in spots]

    def y_pairs(step):
        return [(i, (i + step) % ny) for i in range(ny)]

    z_steps = [s if s <= nz // 2 else s - nz for s in range(1, nz)]
    own = shard_for(0)
    near = [lax.ppermute(shard_for(s), ("zlo", "zhi"), z_pairs(s)) for s in z_steps]
    own_y = [own] + [lax.ppermute(own, "y", y_pairs(s)) for s in range(1, ny)]
    near = jnp.concatenate(near, axis=0)
    near_y = [near] + [lax.ppermute(near, "y", y_pairs(s)) for s in range(1, ny)]
    left = jnp.concatenate([p for pair in zip(own_y, near_y) for p in pair], axis=0)
    right = lax.all_gather(block, "x", axis=0, tiled=True)
    degree_chip = lax.psum(jnp.sum(block.astype(f32), axis=1), "core").reshape(nk, rows_dev)
    degree_own = jnp.where(k_id == 0, degree_chip[0], degree_chip[1])
    spread = jnp.broadcast_to(degree_own[None], (nx * nc, rows_dev))
    degree = lax.all_to_all(spread, ("x", "zlo", "y"), split_axis=0, concat_axis=0, tiled=True)
    scale = 1.0 / degree.reshape(1, half)
    right = (right.astype(f32) * scale).astype(bf16)
    partial = lax.dot_general(left, right, (((1,), (1,)), ((), ())), preferred_element_type=f32)
    partial = partial.reshape(nc, nk, part, nx * BLK)
    mine = jnp.where(k_id == 0, partial[:, 0], partial[:, 1])
    theirs = jnp.where(k_id == 0, partial[:, 1], partial[:, 0])
    summed = mine + lax.ppermute(theirs, "core", [(0, 1), (1, 0)])
    prune = prune_mask.reshape(nc, nx, nc, nx)
    prune = lax.dynamic_index_in_dim(prune, x_id, 1, keepdims=False)
    prune = lax.dynamic_index_in_dim(prune, c_id, 1, keepdims=False)
    steps_z = (lax.axis_index("zlo") - jnp.arange(nz)) % nz
    steps_y = (lax.axis_index("y") - jnp.arange(ny)) % ny
    spot = (steps_y[None, :] * nz + steps_z[:, None]).reshape(nc)
    summed = summed[spot]
    prune = jnp.repeat(prune.astype(f32), BLK, axis=1)
    pruned = summed * summed * prune[:, None, :]
    mass = jnp.sum(pruned, axis=(0, 1))
    for axis in ("core", "x", "zhi"):
        mass = lax.psum(mass, axis)
    return pruned * (node_count / mass)[None, None, :]


def solution(mesh):
    rows, cols, layers = mesh.devices.shape
    devices = mesh.devices.reshape(rows // 2, 2, cols // 4, 4, layers)
    split = Mesh(devices, ("x", "core", "zlo", "y", "zhi"))
    in_specs = (P(("zlo", "y"), ("x", "core"), None), P(), P())
    out_specs = P(None, ("x", "core", "zhi"), ("zlo", "y"))
    return jax.shard_map(
        on_device, mesh=split, in_specs=in_specs, out_specs=out_specs, check_vma=False
    )
```

```python
import functools

import jax
import jax.numpy as jnp
from jax import lax
from jax.experimental import pallas as pl
from jax.experimental.pallas import tpu as pltpu
from jax.sharding import Mesh, PartitionSpec as P

BLK = 128
KB = 512
INTERPRET = False
BF16, F32 = jnp.bfloat16, jnp.float32
PARAMS = dict(vmem_limit_bytes=48 * 1024 * 1024)


def sizes():
    return tuple(lax.axis_size(a) for a in ("x", "core", "zlo", "y", "zhi"))


def col_index():
    return lax.axis_index("zlo") * lax.axis_size("y") + lax.axis_index("y")


def mask_kernel(mask_ref, adj_ref, out_ref):
    nx, nk, nz, ny, nl = sizes()
    nc = nz * ny
    row = col_index() * nx + lax.axis_index("x")
    for c in range(nc):
        for x in range(nx):
            keep = mask_ref[row, c * nx + x].astype(F32).astype(BF16)
            lo = (c * nx + x) * BLK
            out_ref[x * nc + c] = adj_ref[0, :, lo : lo + BLK] * keep


def halves_kernel(out_ref, kept_ref, given_ref):
    n = out_ref.shape[1]
    flip = lax.axis_index("core") == 1
    low = lax.broadcasted_iota(jnp.int32, (n, BLK), 1) < n
    for p in range(out_ref.shape[0] // 2):
        a = out_ref[2 * p].astype(F32)
        b = out_ref[2 * p + 1].astype(F32)
        first = jnp.where(low, a, pltpu.roll(b, n, 1)).astype(BF16)
        second = jnp.where(low, pltpu.roll(a, n, 1), b).astype(BF16)
        cols = slice(p * BLK, (p + 1) * BLK)
        kept_ref[:, cols] = jnp.where(flip, second, first)
        given_ref[:, cols] = jnp.where(flip, first, second)


def form_kernel(recv_ref, kept_ref, other_ref, block_ref, shard_ref, sum_ref, acc_ref):
    nx, nk, nz, ny, nl = sizes()
    nc = nz * ny
    n = kept_ref.shape[0]
    part = n // nl
    step = pl.program_id(0)
    core = lax.axis_index("core")
    c_id = col_index()

    def tile(p):
        flipped = recv_ref[pl.ds(2 * p, 2)].reshape(BLK, BLK).astype(F32).T
        cols = pl.ds(pl.multiple_of(p * BLK, BLK), BLK)
        kept = kept_ref[:, cols].astype(F32)
        other = other_ref[:, cols].astype(F32)
        direct = jnp.concatenate(
            [jnp.where(core == 0, kept, other), jnp.where(core == 0, other, kept)], axis=0
        )
        return direct + flipped, cols

    acc = jnp.zeros((BLK, BLK), F32)
    own_p = jnp.where(step == lax.axis_index("x"), c_id // 2, -1)
    r = lax.broadcasted_iota(jnp.int32, (BLK, BLK), 0)
    k = lax.broadcasted_iota(jnp.int32, (BLK, BLK), 1)
    shift = (c_id % 2 - core) * n
    diagonal = jnp.where((r // n == core) & (k == r + shift), 1.0, 0.0)
    for p in range(nc // 2):
        value, cols = tile(p)
        value = value + jnp.where(own_p == p, diagonal, 0.0)
        rounded = value.astype(BF16)
        block_ref[:, p * BLK : (p + 1) * BLK] = rounded
        acc = acc + rounded.astype(F32)

    @pl.when(step == 0)
    def _():
        acc_ref[...] = acc

    @pl.when(step > 0)
    def _():
        acc_ref[...] += acc

    z_id = lax.axis_index("zhi") * nz + lax.axis_index("zlo")
    for i, s in enumerate(z_steps(nz)):
        layer = (z_id + s + nz * nl) % (nz * nl) // nz
        for half in range(nk):
            rows = pl.ds(pl.multiple_of(half * n + layer * part, part), part)
            shard_ref[i, half * part : (half + 1) * part, :] = block_ref[rows, :]

    @pl.when(step == pl.num_programs(0) - 1)
    def _():
        sum_ref[...] = jnp.sum(acc_ref[...].T, axis=0, keepdims=True)


def z_steps(nz):
    return [s if s <= nz // 2 else s - nz for s in range(nz)]


def product_kernel(own_ref, near_ref, right_ref, degree_ref, mine_ref, theirs_ref, left, acc):
    nx, nk, nz, ny, nl = sizes()
    part = own_ref.shape[1] // nk
    rows = nk * part
    for y in range(ny):
        base = y * nz * rows
        left[base : base + rows, :] = own_ref[y]
        left[base + rows : base + nz * rows, :] = near_ref[y]
    right = (right_ref[...].astype(F32) * (1.0 / degree_ref[...])).astype(BF16)
    value = lax.dot_general(
        left[...], right, (((1,), (1,)), ((), ())), preferred_element_type=F32
    )
    value = value.reshape(acc.shape)

    @pl.when(pl.program_id(0) == 0)
    def _():
        acc[...] = value

    @pl.when(pl.program_id(0) > 0)
    def _():
        acc[...] += value

    @pl.when(pl.program_id(0) == pl.num_programs(0) - 1)
    def _():
        core = lax.axis_index("core")
        for z in range(nz):
            step = (lax.axis_index("zlo") - z + nz) % nz
            for y in range(ny):
                spot = (y * nz + step) * nk
                mine_ref[z * ny + y] = acc[spot + core]
                theirs_ref[z * ny + y] = acc[spot + 1 - core]


def on_device(adjacency, block_mask, prune_mask):
    rows_dev = adjacency.shape[1]
    node_count = adjacency.shape[2]
    nx, nk, nz, ny, nl = sizes()
    nc = nz * ny
    x_id, k_id = lax.axis_index("x"), lax.axis_index("core")
    c_id = col_index()
    part = rows_dev // nl
    half = node_count // nk
    shape = jax.ShapeDtypeStruct
    smem = pl.BlockSpec(memory_space=pltpu.SMEM)
    call = functools.partial(
        pl.pallas_call, compiler_params=pltpu.CompilerParams(**PARAMS), interpret=INTERPRET
    )
    outgoing = call(
        mask_kernel,
        out_shape=shape((nx * nc, rows_dev, BLK), BF16),
        in_specs=[smem, pl.BlockSpec(memory_space=pltpu.VMEM)],
    )(block_mask, adjacency)
    received = lax.all_to_all(outgoing, ("x", "zlo", "y"), split_axis=0, concat_axis=0, tiled=True)
    kept, given = call(halves_kernel, out_shape=[shape((rows_dev, half), BF16)] * 2)(outgoing)
    other = lax.ppermute(given, "core", [(0, 1), (1, 0)])
    width = half // nx
    block, shards, row_sum = call(
        form_kernel,
        grid=(nx,),
        in_specs=[
            pl.BlockSpec((nc, rows_dev, BLK), lambda i: (i, 0, 0)),
            pl.BlockSpec((rows_dev, width), lambda i: (0, i)),
            pl.BlockSpec((rows_dev, width), lambda i: (0, i)),
        ],
        out_specs=[
            pl.BlockSpec((BLK, width), lambda i: (0, i)),
            pl.BlockSpec((nz, nk * part, width), lambda i: (0, 0, i)),
            pl.BlockSpec((1, BLK), lambda i: (0, 0)),
        ],
        out_shape=[
            shape((BLK, half), BF16),
            shape((nz, nk * part, half), BF16),
            shape((1, BLK), F32),
        ],
        scratch_shapes=[pltpu.VMEM((BLK, BLK), F32)],
    )(received, kept, other)

    def z_pairs(step):
        spots = [(z, (z + step) % (nz * nl)) for z in range(nz * nl)]
        return [(a % nz * nl + a // nz, b % nz * nl + b // nz) for a, b in spots]

    def spread(piece, axes, count):
        wide = jnp.broadcast_to(piece[None], (count,) + piece.shape)
        return lax.all_to_all(wide, axes, split_axis=0, concat_axis=0, tiled=True)

    near = [
        lax.ppermute(shards[i], ("zlo", "zhi"), z_pairs(s))
        for i, s in enumerate(z_steps(nz))
        if i > 0
    ]
    own_y = spread(shards[0], "y", ny)
    near_y = spread(jnp.concatenate(near, axis=0), "y", ny)
    right = lax.all_gather(block, "x", axis=0, tiled=True)
    degree_chip = lax.psum(row_sum, "core").reshape(nk, rows_dev)
    degree_own = jnp.where(k_id == 0, degree_chip[0], degree_chip[1])
    degree = spread(degree_own, ("x", "zlo", "y"), nx * nc).reshape(1, half)
    tile_cols = nx * BLK
    mine, theirs = call(
        product_kernel,
        grid=(half // KB,),
        in_specs=[
            pl.BlockSpec((ny, nk * part, KB), lambda i: (0, 0, i)),
            pl.BlockSpec((ny, (nz - 1) * nk * part, KB), lambda i: (0, 0, i)),
            pl.BlockSpec((tile_cols, KB), lambda i: (0, i)),
            pl.BlockSpec((1, KB), lambda i: (0, i)),
        ],
        out_specs=[pl.BlockSpec((nc, part, tile_cols), lambda i: (0, 0, 0))] * 2,
        out_shape=[shape((nc, part, tile_cols), F32)] * 2,
        scratch_shapes=[
            pltpu.VMEM((nc * nk * part, KB), BF16),
            pltpu.VMEM((nc * nk, part, tile_cols), F32),
        ],
    )(own_y, near_y, right, degree)
    summed = mine + lax.ppermute(theirs, "core", [(0, 1), (1, 0)])
    prune = prune_mask.reshape(nc, nx, nc, nx)
    prune = lax.dynamic_index_in_dim(prune, x_id, 1, keepdims=False)
    prune = lax.dynamic_index_in_dim(prune, c_id, 1, keepdims=False)
    prune = jnp.repeat(prune.astype(F32), BLK, axis=1)
    pruned = summed * summed * prune[:, None, :]
    mass = lax.psum(jnp.sum(pruned, axis=(0, 1)), "core")
    mass = jnp.sum(spread(mass.reshape(-1, BLK), ("x", "zhi"), nx * nl), axis=0).reshape(-1)
    return pruned * (node_count / mass)[None, None, :]


def solution(mesh):
    rows, cols, layers = mesh.devices.shape
    devices = mesh.devices.reshape(rows // 2, 2, cols // 4, 4, layers)
    split = Mesh(devices, ("x", "core", "zlo", "y", "zhi"))
    in_specs = (P(("zlo", "y"), ("x", "core"), None), P(), P())
    out_specs = P(None, ("x", "core", "zhi"), ("zlo", "y"))
    return jax.shard_map(
        on_device, mesh=split, in_specs=in_specs, out_specs=out_specs, check_vma=False
    )
```

```python
import functools

import jax
import jax.numpy as jnp
from jax import lax
from jax.experimental import pallas as pl
from jax.experimental.pallas import tpu as pltpu
from jax.sharding import Mesh, PartitionSpec as P

BLK = 128
KB = 512
INTERPRET = False
BF16, F32 = jnp.bfloat16, jnp.float32
PARAMS = dict(vmem_limit_bytes=48 * 1024 * 1024)
AXES = ("x", "core", "zlo", "y1", "y0", "zhi")
SWAP = [(0, 1), (1, 0)]


def where_am_i():
    return tuple(lax.axis_index(a) for a in AXES)


def z_steps(nz):
    return [s if s <= nz // 2 else s - nz for s in range(nz)]


def mask_kernel(mask_ref, adj_ref, out_ref):
    x_id, _, z_id, y1, y0, _ = where_am_i()
    nx, nz = lax.axis_size("x"), lax.axis_size("zlo")
    row = (z_id * 4 + y1 * 2 + y0) * nx + x_id
    for x in range(nx):
        for z in range(nz):
            base = (x * nz + z) * 2
            for y in range(4):
                block = (z * 4 + y) * nx + x
                keep = mask_ref[row, block].astype(F32).astype(BF16)
                low, high = (y, 0) if y < 2 else (3 - y, 1)
                spot = base + jnp.where(y1 == 0, low, 1 - low)
                out_ref[spot, :, high * BLK : (high + 1) * BLK] = (
                    adj_ref[0, :, block * BLK : (block + 1) * BLK] * keep
                )


def pieces_kernel(out_ref, piece_ref):
    _, core, _, y1, _, _ = where_am_i()
    n = out_ref.shape[1]
    low_lanes = lax.broadcasted_iota(jnp.int32, (n, BLK), 1) < n
    for p in range(out_ref.shape[0] // 2):
        cols = slice(p * BLK, (p + 1) * BLK)
        outer = out_ref[2 * p + y1].astype(F32)
        inner = out_ref[2 * p + 1 - y1].astype(F32)
        tiles = [outer[:, :BLK], inner[:, :BLK], inner[:, BLK:], outer[:, BLK:]]
        for half in range(2):
            a, b = tiles[2 * half], tiles[2 * half + 1]
            first = jnp.where(low_lanes, a, pltpu.roll(b, n, 1)).astype(BF16)
            second = jnp.where(low_lanes, pltpu.roll(a, n, 1), b).astype(BF16)
            i = jnp.where(y1 == half, 0, 1)
            piece_ref[2 * i + core, :, cols] = first
            piece_ref[2 * i + 1 - core, :, cols] = second


def form_kernel(recv_ref, d00, d01, d10, d11, block_ref, shard_ref, sum_ref, flip_ref, acc_ref):
    x_id, core, z_id, y1, y0, l_id = where_am_i()
    nz, nl = lax.axis_size("zlo"), lax.axis_size("zhi")
    n = d00.shape[0]
    part = n // nl
    step = pl.program_id(0)
    own_p = jnp.where(step == x_id, z_id, -1)
    r = lax.broadcasted_iota(jnp.int32, (n, BLK), 0)
    k = lax.broadcasted_iota(jnp.int32, (n, BLK), 1)
    diagonal = jnp.where(k == r + y0 * n, 1.0, 0.0)

    @pl.when(step == 0)
    def _():
        acc_ref[...] = jnp.zeros_like(acc_ref)

    for p in range(nz):
        cols = slice(p * BLK, (p + 1) * BLK)
        got = recv_ref[2 * p : 2 * p + 2].reshape(BLK, 2 * BLK).astype(F32)
        flip_ref[...] = got.T.reshape(flip_ref.shape)
        for i, direct in enumerate((d00, d01, d10, d11)):
            b, c = i // 2, i % 2
            spot = jnp.where(y1 == b, 0, 2) + jnp.where(core == c, 0, 1)
            value = direct[:, cols].astype(F32) + flip_ref[spot]
            if i == 0:
                value = value + jnp.where(own_p == p, diagonal, 0.0)
            rounded = value.astype(BF16)
            block_ref[spot, :, cols] = rounded
            acc_ref[spot] += rounded.astype(F32)

    z_pos = l_id * nz + z_id
    for i, s in enumerate(z_steps(nz)):
        layer = (z_pos + s + nz * nl) % (nz * nl) // nz
        rows = pl.ds(pl.multiple_of(layer * part, part), part)
        for group in range(4):
            shard_ref[i, group * part : (group + 1) * part, :] = block_ref[group, rows, :]

    @pl.when(step == pl.num_programs(0) - 1)
    def _():
        acc = acc_ref[...].reshape(4 * n, BLK)
        sum_ref[...] = jnp.sum(acc.T, axis=0, keepdims=True)


def product_kernel(
    own_ref, far_ref, right_ref, degree_ref, m_own, m_oth, t_own, t_oth, left, right, acc
):
    _, core, z_id, y1, y0, _ = where_am_i()
    nx, nz, nl = lax.axis_size("x"), lax.axis_size("zlo"), lax.axis_size("zhi")
    rows = own_ref.shape[0]
    left[:rows] = own_ref[...]
    left[rows:] = far_ref[...]
    inverse = 1.0 / degree_ref[...]
    for x in range(nx):
        for b in range(2):
            spot = jnp.where(y1 == b, 0, nx) + x
            scaled = right_ref[2 * x + b].astype(F32) * inverse
            right[spot] = scaled.astype(BF16)
    value = lax.dot_general(
        left[...],
        right[...].reshape(-1, right.shape[2]),
        (((1,), (1,)), ((), ())),
        preferred_element_type=F32,
    )
    value = value.reshape(acc.shape)

    @pl.when(pl.program_id(0) == 0)
    def _():
        acc[...] = value

    @pl.when(pl.program_id(0) > 0)
    def _():
        acc[...] += value

    @pl.when(pl.program_id(0) == pl.num_programs(0) - 1)
    def _():
        width = nx * BLK
        for z in range(nz):
            step = (z_id - z + nz) % nz
            for y in range(4):
                low, b = (y, 0) if y < 2 else (3 - y, 1)
                far = jnp.where((y0 + y1) % 2 == low, 0, 1)
                spot = ((far * nz + step) * 2 + b) * 2
                m_own[z * 4 + y] = acc[spot + core, :, :width]
                m_oth[z * 4 + y] = acc[spot + core, :, width:]
                t_own[z * 4 + y] = acc[spot + 1 - core, :, :width]
                t_oth[z * 4 + y] = acc[spot + 1 - core, :, width:]


def on_device(adjacency, block_mask, prune_mask):
    rows_dev = adjacency.shape[1]
    node_count = adjacency.shape[2]
    nx, nk, nz, _, _, nl = (lax.axis_size(a) for a in AXES)
    nc = nz * 4
    x_id, k_id, z_id, y1, y0, _ = where_am_i()
    c_id = z_id * 4 + y1 * 2 + y0
    part = rows_dev // nl
    inner = node_count // 4
    width = inner // nx
    shape = jax.ShapeDtypeStruct
    vmem = pl.BlockSpec(memory_space=pltpu.VMEM)
    call = functools.partial(
        pl.pallas_call, compiler_params=pltpu.CompilerParams(**PARAMS), interpret=INTERPRET
    )
    group = ("x", "zlo", "y0")
    members = nx * nz * 2

    def partner(value):
        return lax.ppermute(value, ("y1", "y0"), [(y, 3 - y) for y in range(4)])

    def other_core(value):
        return lax.ppermute(value, "core", SWAP)

    def spread(piece, axes, count):
        wide = jnp.broadcast_to(piece[None], (count,) + piece.shape)
        return lax.all_to_all(wide, axes, split_axis=0, concat_axis=0, tiled=True)

    outgoing = call(
        mask_kernel,
        out_shape=shape((members, rows_dev, 2 * BLK), BF16),
        in_specs=[pl.BlockSpec(memory_space=pltpu.SMEM), vmem],
        out_specs=vmem,
    )(block_mask, adjacency)
    received = lax.all_to_all(outgoing, group, split_axis=0, concat_axis=0, tiled=True)
    pieces = call(pieces_kernel, out_shape=shape((4, rows_dev, inner), BF16))(outgoing)
    across = [(c * 4 + y, (1 - c) * 4 + 3 - y) for c in range(2) for y in range(4)]
    direct = [
        pieces[0],
        other_core(pieces[1]),
        partner(pieces[2]),
        lax.ppermute(pieces[3], ("core", "y1", "y0"), across),
    ]
    block, shards, row_sum = call(
        form_kernel,
        grid=(nx,),
        in_specs=[pl.BlockSpec((2 * nz, rows_dev, 2 * BLK), lambda i: (i, 0, 0))]
        + [pl.BlockSpec((rows_dev, width), lambda i: (0, i))] * 4,
        out_specs=[
            pl.BlockSpec((4, rows_dev, width), lambda i: (0, 0, i)),
            pl.BlockSpec((nz, 4 * part, width), lambda i: (0, 0, i)),
            pl.BlockSpec((1, 4 * rows_dev), lambda i: (0, 0)),
        ],
        out_shape=[
            shape((4, rows_dev, inner), BF16),
            shape((nz, 4 * part, inner), BF16),
            shape((1, 4 * rows_dev), F32),
        ],
        scratch_shapes=[
            pltpu.VMEM((4, rows_dev, BLK), F32),
            pltpu.VMEM((4, rows_dev, BLK), F32),
        ],
    )(received, *direct)

    def z_pairs(step):
        spots = [(z, (z + step) % (nz * nl)) for z in range(nz * nl)]
        return [(a % nz * nl + a // nz, b % nz * nl + b // nz) for a, b in spots]

    near = [
        lax.ppermute(shards[i], ("zlo", "zhi"), z_pairs(s)) if i else shards[0]
        for i, s in enumerate(z_steps(nz))
    ]
    own_rows = jnp.concatenate(near, axis=0)
    far_rows = lax.ppermute(own_rows, "y0", SWAP)
    right = lax.all_gather(block.reshape(4 * rows_dev, inner), "x", axis=0, tiled=True)
    degree_pair = lax.psum(row_sum, "core")
    degree_pair = (degree_pair + partner(degree_pair)).reshape(4, rows_dev)
    degree_own = lax.dynamic_index_in_dim(degree_pair, y1 * 2 + k_id, 0, keepdims=False)
    degree = spread(degree_own, group, members).reshape(1, inner)
    tile_cols = nx * BLK
    tile = shape((nc, part, tile_cols), F32)
    m_own, m_oth, t_own, t_oth = call(
        product_kernel,
        grid=(inner // KB,),
        in_specs=[
            pl.BlockSpec((nz * 4 * part, KB), lambda i: (0, i)),
            pl.BlockSpec((nz * 4 * part, KB), lambda i: (0, i)),
            pl.BlockSpec((2 * nx, BLK, KB), lambda i: (0, 0, i)),
            pl.BlockSpec((1, KB), lambda i: (0, i)),
        ],
        out_specs=[pl.BlockSpec(tile.shape, lambda i: (0, 0, 0))] * 4,
        out_shape=[tile] * 4,
        scratch_shapes=[
            pltpu.VMEM((2 * nz * 4 * part, KB), BF16),
            pltpu.VMEM((2 * nx, BLK, KB), BF16),
            pltpu.VMEM((2 * nc, part, 2 * tile_cols), F32),
        ],
    )(own_rows, far_rows, right.reshape(2 * nx, BLK, inner), degree)
    sent = (m_oth + other_core(t_oth)).astype(BF16)
    summed = m_own + other_core(t_own) + partner(sent).astype(F32)
    prune = prune_mask.reshape(nc, nx, nc, nx)
    prune = lax.dynamic_index_in_dim(prune, x_id, 1, keepdims=False)
    prune = lax.dynamic_index_in_dim(prune, c_id, 1, keepdims=False)
    prune = jnp.repeat(prune.astype(F32), BLK, axis=1)
    pruned = summed * summed * prune[:, None, :]
    mass = lax.psum(jnp.sum(pruned, axis=(0, 1)), "core")
    mass = jnp.sum(spread(mass.reshape(-1, BLK), ("x", "zhi"), nx * nl), axis=0).reshape(-1)
    return pruned * (node_count / mass)[None, None, :]


def solution(mesh):
    rows, cols, layers = mesh.devices.shape
    devices = mesh.devices.reshape(rows // 2, 2, cols // 4, 2, 2, layers)
    split = Mesh(devices, AXES)
    in_specs = (P(("zlo", "y1", "y0"), ("x", "core"), None), P(), P())
    out_specs = P(None, ("x", "core", "zhi"), ("zlo", "y1", "y0"))
    return jax.shard_map(
        on_device, mesh=split, in_specs=in_specs, out_specs=out_specs, check_vma=False
    )
```

```python
import functools

import jax
import jax.numpy as jnp
from jax import lax
from jax.experimental import pallas as pl
from jax.experimental.pallas import tpu as pltpu
from jax.sharding import Mesh, PartitionSpec as P

BLK = 128
INTERPRET = False
BF16, F32 = jnp.bfloat16, jnp.float32
PARAMS = dict(vmem_limit_bytes=48 * 1024 * 1024)
AXES = ("x", "core", "z1", "z0", "y", "zhi")
SWAP = [(0, 1), (1, 0)]


def where_am_i():
    return tuple(lax.axis_index(a) for a in AXES)


def mask_kernel(mask_ref, adj_ref, out_ref):
    x_id, _, z1, z0, y_id, _ = where_am_i()
    nx, ny = lax.axis_size("x"), lax.axis_size("y")
    row = ((z1 * 2 + z0) * ny + y_id) * nx + x_id
    for x in range(nx):
        for z in range(4):
            low, high = (z, 0) if z < 2 else (3 - z, 1)
            base = (x * 2 + jnp.where(z1 == 0, low, 1 - low)) * ny
            for y in range(ny):
                block = (z * ny + y) * nx + x
                keep = mask_ref[row, block].astype(F32).astype(BF16)
                out_ref[base + y, :, high * BLK : (high + 1) * BLK] = (
                    adj_ref[0, :, block * BLK : (block + 1) * BLK] * keep
                )


def pieces_kernel(out_ref, piece_ref):
    _, core, z1, _, _, _ = where_am_i()
    nx, ny = lax.axis_size("x"), lax.axis_size("y")
    n = out_ref.shape[1]
    low_lanes = lax.broadcasted_iota(jnp.int32, (n, BLK), 1) < n
    for p in range(nx * ny):
        x, z0, q = p // ny, p % ny // (ny // 2), p % (ny // 2)
        cols = slice(p * BLK, (p + 1) * BLK)
        for half in range(2):
            low = z0 ^ half
            spot = (x * 2 + jnp.where(z1 == 0, low, 1 - low)) * ny + 2 * q
            lanes = slice(half * BLK, (half + 1) * BLK)
            a = out_ref[spot, :, lanes].astype(F32)
            b = out_ref[spot + 1, :, lanes].astype(F32)
            first = jnp.where(low_lanes, a, pltpu.roll(b, n, 1)).astype(BF16)
            second = jnp.where(low_lanes, pltpu.roll(a, n, 1), b).astype(BF16)
            i = jnp.where(z1 == half, 0, 1)
            piece_ref[2 * i + core, :, cols] = first
            piece_ref[2 * i + 1 - core, :, cols] = second


def form_kernel(
    recv_ref, d00, d01, d10, d11, block_ref, shard_ref, sum_ref, flip_ref, acc_ref
):
    x_id, core, z1, z0, y_id, l_id = where_am_i()
    ny, nl = lax.axis_size("y"), lax.axis_size("zhi")
    n = d00.shape[0]
    part = n // nl
    step = pl.program_id(0)
    own_source = z0 * ny + y_id
    own_p = jnp.where(step == x_id, own_source // 2, -1)
    r = lax.broadcasted_iota(jnp.int32, (n, BLK), 0)
    k = lax.broadcasted_iota(jnp.int32, (n, BLK), 1)
    diagonal = jnp.where(k == r + own_source % 2 * n, 1.0, 0.0)

    @pl.when(step == 0)
    def _():
        acc_ref[...] = jnp.zeros_like(acc_ref)

    for p in range(ny):
        cols = slice(p * BLK, (p + 1) * BLK)
        got = recv_ref[2 * p : 2 * p + 2].reshape(BLK, 2 * BLK).astype(F32)
        flip_ref[...] = got.T.reshape(flip_ref.shape)
        for i, direct in enumerate((d00, d01, d10, d11)):
            b, c = i // 2, i % 2
            spot = jnp.where(z1 == b, 0, 2) + jnp.where(core == c, 0, 1)
            value = direct[:, cols].astype(F32) + flip_ref[spot]
            if i == 0:
                value = value + jnp.where(own_p == p, diagonal, 0.0)
            rounded = value.astype(BF16)
            block_ref[2 * jnp.where(core == c, 0, 1) + b, :, cols] = rounded
            acc_ref[spot] += rounded.astype(F32)

    rows = pl.ds(pl.multiple_of(l_id * part, part), part)
    for group in range(4):
        spot = group % 2 * 2 + (group // 2 ^ z1)
        shard_ref[group * part : (group + 1) * part, :] = block_ref[spot, rows, :]

    @pl.when(step == pl.num_programs(0) - 1)
    def _():
        acc = acc_ref[...].reshape(4 * n, BLK)
        sum_ref[...] = jnp.sum(acc.T, axis=0, keepdims=True)


def product_kernel(group, left_ref, *refs):
    *right_refs, degree_ref, mine_ref, theirs_ref, right = refs
    if len(right_refs) == 5:
        own_ref, before_ref, far0_ref, far1_ref, after_ref = right_refs
        right_refs = [(own_ref,) * 2, (before_ref,) * 2, (far0_ref, far1_ref), (after_ref,) * 2]
    else:
        right_refs = [(ref,) * 2 for ref in right_refs]
    x_id, core, z1, _, _, _ = where_am_i()
    nx, ny = lax.axis_size("x"), lax.axis_size("y")
    part = left_ref.shape[0] // (8 * ny)
    inverse = 1.0 / degree_ref[...]
    n = BLK // 2
    for d, pair in enumerate(right_refs):
        for core_rows, ref in enumerate(pair):
            low = (2 * core_rows if ref.shape[0] > BLK else 0) * n + group * n
            block = ref[low : low + n, :].astype(F32)
            rows = slice(d * BLK + core_rows * n, d * BLK + (core_rows + 1) * n)
            right[rows, :] = (block * inverse).astype(BF16)
    value = lax.dot_general(
        left_ref[...], right[...], (((1,), (1,)), ((), ())), preferred_element_type=F32
    )
    value = value.reshape(8 * ny, part, right.shape[0])
    for sel in range(2):
        low = jnp.where(z1 == sel, 0, 1)
        for y in range(ny):
            for b in range(2):
                c = jnp.where(b == 0, low, 3 - low) * ny + y
                spot = ((sel * ny + y) * 2 + b) * 2
                first, second = value[spot], value[spot + 1]
                mine = jnp.where(core == 0, first, second)
                theirs = jnp.where(core == 0, second, first).astype(BF16)
                for e in range(nx):
                    x = (x_id - e + nx) % nx
                    lanes = pl.ds(pl.multiple_of(x * BLK, BLK), BLK)
                    mine_ref[c, :, lanes] = mine[:, e * BLK : (e + 1) * BLK]
                    theirs_ref[c, :, lanes] = theirs[:, e * BLK : (e + 1) * BLK]


def on_device(adjacency, block_mask, prune_mask):
    rows_dev = adjacency.shape[1]
    node_count = adjacency.shape[2]
    nx, nk, _, _, ny, nl = (lax.axis_size(a) for a in AXES)
    nc = 4 * ny
    x_id, k_id, z1, z0, y_id, _ = where_am_i()
    c_id = (z1 * 2 + z0) * ny + y_id
    part = rows_dev // nl
    inner = node_count // 4
    width = inner // nx
    shape = jax.ShapeDtypeStruct
    vmem = pl.BlockSpec(memory_space=pltpu.VMEM)
    params = pltpu.CompilerParams(**PARAMS)
    call = functools.partial(pl.pallas_call, compiler_params=params, interpret=INTERPRET)
    group = ("x", "z0", "y")
    members = nx * 2 * ny

    def other_core(value):
        return lax.ppermute(value, "core", SWAP)

    def spread(piece, axes, count):
        wide = jnp.broadcast_to(piece[None], (count,) + piece.shape)
        return lax.all_to_all(wide, axes, split_axis=0, concat_axis=0, tiled=True)

    ring = []
    for l in range(nl):
        ring += [(0 * nl + l, 3 * nl + (l - 1) % nl), (3 * nl + l, 0 * nl + (l + 1) % nl)]
        ring += [(1 * nl + l, 2 * nl + l), (2 * nl + l, 1 * nl + l)]
    spots = 4 * nl
    ring_across = [(c * spots + a, (1 - c) * spots + b) for c in range(2) for a, b in ring]

    outgoing = call(
        mask_kernel,
        out_shape=shape((members, rows_dev, 2 * BLK), BF16),
        in_specs=[pl.BlockSpec(memory_space=pltpu.SMEM), vmem],
        out_specs=vmem,
    )(block_mask, adjacency)
    received = lax.all_to_all(outgoing, group, split_axis=0, concat_axis=0, tiled=True)
    pieces = call(pieces_kernel, out_shape=shape((4, rows_dev, inner), BF16))(outgoing)
    by_ring = lax.ppermute(pieces[2], ("z1", "z0", "zhi"), ring)
    across = lax.ppermute(pieces[3], ("core", "z1", "z0", "zhi"), ring_across)
    by_ring, swapped = lax.optimization_barrier((by_ring, pieces[1]))
    direct = [pieces[0], other_core(swapped), by_ring, across]
    block, shard, row_sum = call(
        form_kernel,
        grid=(nx,),
        in_specs=[pl.BlockSpec((2 * ny, rows_dev, 2 * BLK), lambda i: (i, 0, 0))]
        + [pl.BlockSpec((rows_dev, width), lambda i: (0, i))] * 4,
        out_specs=[
            pl.BlockSpec((4, rows_dev, width), lambda i: (0, 0, i)),
            pl.BlockSpec((4 * part, width), lambda i: (0, i)),
            pl.BlockSpec((1, 4 * rows_dev), lambda i: (0, 0)),
        ],
        out_shape=[
            shape((4, rows_dev, inner), BF16),
            shape((4 * part, inner), BF16),
            shape((1, 4 * rows_dev), F32),
        ],
        scratch_shapes=[
            pltpu.VMEM((4, rows_dev, BLK), F32),
            pltpu.VMEM((4, rows_dev, BLK), F32),
        ],
    )(received, *direct)
    rows = lax.all_gather(shard, ("z0", "y"), axis=0, tiled=True)
    def step_x(piece, d):
        return lax.ppermute(piece, "x", [(i, (i + d) % nx) for i in range(nx)])

    partial = row_sum.reshape(2, 2, rows_dev).transpose(1, 0, 2)
    partial = jnp.broadcast_to(partial[:, :, None, None], (2, 2, 2, ny, rows_dev))
    partial = lax.all_to_all(
        partial.reshape(8 * ny, rows_dev),
        ("core", "z1", "z0", "y"),
        split_axis=0,
        concat_axis=0,
        tiled=True,
    )
    own_block = block.reshape(2 * BLK, inner)
    blocks = [own_block, step_x(own_block, 1)]
    if nx == 4:
        after = step_x(own_block, -1)
        before, after, partial = lax.optimization_barrier((blocks[1], after, partial))
        blocks = [own_block, before, step_x(before[:BLK], 1), step_x(after[BLK:], -1), after]
    partial = jnp.sum(partial.reshape(2, 2, 2, ny, rows_dev), axis=0)
    degree = jnp.where(
        z1 == 0, partial[0] + partial[1, ::-1], partial[1] + partial[0, ::-1]
    )
    degree = spread(degree.reshape(-1, BLK), "x", nx).reshape(1, inner)
    tile_cols = nx * BLK

    def product(group):
        return call(
            functools.partial(product_kernel, group),
            in_specs=[vmem] * (len(blocks) + 2),
            out_specs=[vmem] * 2,
            out_shape=[shape((nc, part, tile_cols), t) for t in (F32, BF16)],
            scratch_shapes=[pltpu.VMEM((tile_cols, inner), BF16)],
        )(rows, *blocks, degree)

    mine, theirs = product(1)
    sent = (mine + other_core(theirs).astype(F32)).astype(BF16)
    got = lax.all_to_all(
        jnp.stack([sent, sent]),
        ("z1", "z0"),
        split_axis=0,
        concat_axis=0,
        tiled=True,
        axis_index_groups=[[0, 3], [1, 2]],
    )
    got = lax.dynamic_index_in_dim(got, 1 - z1, 0, keepdims=False)
    mine, theirs = product(0)
    summed = mine + other_core(theirs).astype(F32) + got.astype(F32)
    prune = prune_mask.reshape(nc, nx, nc, nx)
    prune = lax.dynamic_index_in_dim(prune, x_id, 1, keepdims=False)
    prune = lax.dynamic_index_in_dim(prune, c_id, 1, keepdims=False)
    prune = jnp.repeat(prune.astype(F32), BLK, axis=1)
    pruned = summed * summed * prune[:, None, :]
    mass = lax.psum(jnp.sum(pruned, axis=(0, 1)), "core")
    mass = jnp.sum(spread(mass.reshape(-1, BLK), ("x", "zhi"), nx * nl), axis=0).reshape(-1)
    return pruned * (node_count / mass)[None, None, :]


def solution(mesh):
    rows, cols, layers = mesh.devices.shape
    devices = mesh.devices.reshape(rows // 2, 2, 2, 2, cols // 4, layers)
    split = Mesh(devices, AXES)
    in_specs = (P(("z1", "z0", "y"), ("x", "core"), None), P(), P())
    out_specs = P(None, ("x", "core", "zhi"), ("z1", "z0", "y"))
    return jax.shard_map(
        on_device, mesh=split, in_specs=in_specs, out_specs=out_specs, check_vma=False
    )
```

```python
import functools

import jax
import jax.numpy as jnp
from jax import lax
from jax.experimental import pallas as pl
from jax.experimental.pallas import tpu as pltpu
from jax.sharding import Mesh, PartitionSpec as P

BLK = 128
INTERPRET = False
BF16, F32 = jnp.bfloat16, jnp.float32
PARAMS = dict(vmem_limit_bytes=48 * 1024 * 1024)
AXES = ("x", "core", "z1", "z0", "y", "zhi")
SWAP = [(0, 1), (1, 0)]


def where_am_i():
    return tuple(lax.axis_index(a) for a in AXES)


def mask_kernel(mask_ref, adj_ref, out_ref):
    x_id, _, z1, z0, y_id, _ = where_am_i()
    nx, ny = lax.axis_size("x"), lax.axis_size("y")
    row = ((z1 * 2 + z0) * ny + y_id) * nx + x_id
    for x in range(nx):
        for z in range(4):
            low, high = (z, 0) if z < 2 else (3 - z, 1)
            base = (x * 2 + jnp.where(z1 == 0, low, 1 - low)) * ny
            for y in range(ny):
                block = (z * ny + y) * nx + x
                keep = mask_ref[row, block].astype(F32).astype(BF16)
                out_ref[base + y, :, high * BLK : (high + 1) * BLK] = (
                    adj_ref[0, :, block * BLK : (block + 1) * BLK] * keep
                )


def pieces_kernel(out_ref, piece_ref):
    _, core, z1, _, _, _ = where_am_i()
    nx, ny = lax.axis_size("x"), lax.axis_size("y")
    n = out_ref.shape[1]
    low_lanes = lax.broadcasted_iota(jnp.int32, (n, BLK), 1) < n
    for p in range(nx * ny):
        x, z0, q = p // ny, p % ny // (ny // 2), p % (ny // 2)
        cols = slice(p * BLK, (p + 1) * BLK)
        for half in range(2):
            low = z0 ^ half
            spot = (x * 2 + jnp.where(z1 == 0, low, 1 - low)) * ny + 2 * q
            lanes = slice(half * BLK, (half + 1) * BLK)
            a = out_ref[spot, :, lanes].astype(F32)
            b = out_ref[spot + 1, :, lanes].astype(F32)
            first = jnp.where(low_lanes, a, pltpu.roll(b, n, 1)).astype(BF16)
            second = jnp.where(low_lanes, pltpu.roll(a, n, 1), b).astype(BF16)
            i = jnp.where(z1 == half, 0, 1)
            piece_ref[2 * i + core, :, cols] = first
            piece_ref[2 * i + 1 - core, :, cols] = second


def form_kernel(
    recv_ref, d00, d01, d10, d11, block_ref, shard_ref, sum_ref, flip_ref, acc_ref
):
    x_id, core, z1, z0, y_id, l_id = where_am_i()
    ny, nl = lax.axis_size("y"), lax.axis_size("zhi")
    n = d00.shape[0]
    part = n // nl
    step = pl.program_id(0)
    own_source = z0 * ny + y_id
    own_p = jnp.where(step == x_id, own_source // 2, -1)
    r = lax.broadcasted_iota(jnp.int32, (n, BLK), 0)
    k = lax.broadcasted_iota(jnp.int32, (n, BLK), 1)
    diagonal = jnp.where(k == r + own_source % 2 * n, 1.0, 0.0)

    @pl.when(step == 0)
    def _():
        acc_ref[...] = jnp.zeros_like(acc_ref)

    for p in range(ny):
        cols = slice(p * BLK, (p + 1) * BLK)
        got = recv_ref[2 * p : 2 * p + 2].reshape(BLK, 2 * BLK).astype(F32)
        flip_ref[...] = got.T.reshape(flip_ref.shape)
        for i, direct in enumerate((d00, d01, d10, d11)):
            b, c = i // 2, i % 2
            spot = jnp.where(z1 == b, 0, 2) + jnp.where(core == c, 0, 1)
            value = direct[:, cols].astype(F32) + flip_ref[spot]
            if i == 0:
                value = value + jnp.where(own_p == p, diagonal, 0.0)
            rounded = value.astype(BF16)
            block_ref[2 * jnp.where(core == c, 0, 1) + b, :, cols] = rounded
            acc_ref[spot] += rounded.astype(F32)

    rows = pl.ds(pl.multiple_of(l_id * part, part), part)
    for group in range(4):
        spot = group % 2 * 2 + (group // 2 ^ z1)
        shard_ref[group * part : (group + 1) * part, :] = block_ref[spot, rows, :]

    @pl.when(step == pl.num_programs(0) - 1)
    def _():
        acc = acc_ref[...].reshape(4 * n, BLK)
        sum_ref[...] = jnp.sum(acc.T, axis=0, keepdims=True)


def product_kernel(group, ny, *refs):
    left_refs, refs = refs[:ny], refs[ny:]
    *right_refs, degree_ref, mine_ref, theirs_ref, left, right = refs
    if len(right_refs) == 5:
        own_ref, before_ref, far0_ref, far1_ref, after_ref = right_refs
        right_refs = [(own_ref,) * 2, (before_ref,) * 2, (far0_ref, far1_ref), (after_ref,) * 2]
    else:
        right_refs = [(ref,) * 2 for ref in right_refs]
    x_id, core, z1, z0, y_id, _ = where_am_i()
    nx = lax.axis_size("x")
    lines = left_refs[0].shape[0]
    part = lines // 8
    for i, ref in enumerate(left_refs):
        left[i * lines : (i + 1) * lines, :] = ref[...]
    inverse = 1.0 / degree_ref[...]
    n = BLK // 2
    for d, pair in enumerate(right_refs):
        for core_rows, ref in enumerate(pair):
            low = (2 * core_rows if ref.shape[0] > BLK else 0) * n + group * n
            block = ref[low : low + n, :].astype(F32)
            rows = slice(d * BLK + core_rows * n, d * BLK + (core_rows + 1) * n)
            right[rows, :] = (block * inverse).astype(BF16)
    value = lax.dot_general(
        left[...], right[...], (((1,), (1,)), ((), ())), preferred_element_type=F32
    )
    value = value.reshape(8 * ny, part, right.shape[0])
    for sel in range(2):
        low = jnp.where((z0 + z1) % 2 == sel, 0, 1)
        for y in range(ny):
            for b in range(2):
                c = jnp.where(b == 0, low, 3 - low) * ny + (y_id - y + ny) % ny
                spot = ((y * 2 + sel) * 2 + b) * 2
                first, second = value[spot], value[spot + 1]
                mine = jnp.where(core == 0, first, second)
                theirs = jnp.where(core == 0, second, first).astype(BF16)
                for e in range(nx):
                    x = (x_id - e + nx) % nx
                    lanes = pl.ds(pl.multiple_of(x * BLK, BLK), BLK)
                    mine_ref[c, :, lanes] = mine[:, e * BLK : (e + 1) * BLK]
                    theirs_ref[c, :, lanes] = theirs[:, e * BLK : (e + 1) * BLK]


def on_device(adjacency, block_mask, prune_mask):
    rows_dev = adjacency.shape[1]
    node_count = adjacency.shape[2]
    nx, nk, _, _, ny, nl = (lax.axis_size(a) for a in AXES)
    nc = 4 * ny
    x_id, k_id, z1, z0, y_id, _ = where_am_i()
    c_id = (z1 * 2 + z0) * ny + y_id
    part = rows_dev // nl
    inner = node_count // 4
    width = inner // nx
    shape = jax.ShapeDtypeStruct
    vmem = pl.BlockSpec(memory_space=pltpu.VMEM)
    params = pltpu.CompilerParams(**PARAMS)
    call = functools.partial(pl.pallas_call, compiler_params=params, interpret=INTERPRET)
    group = ("x", "z0", "y")
    members = nx * 2 * ny

    def other_core(value):
        return lax.ppermute(value, "core", SWAP)

    def spread(piece, axes, count):
        wide = jnp.broadcast_to(piece[None], (count,) + piece.shape)
        return lax.all_to_all(wide, axes, split_axis=0, concat_axis=0, tiled=True)

    ring = []
    for l in range(nl):
        ring += [(0 * nl + l, 3 * nl + (l - 1) % nl), (3 * nl + l, 0 * nl + (l + 1) % nl)]
        ring += [(1 * nl + l, 2 * nl + l), (2 * nl + l, 1 * nl + l)]
    spots = 4 * nl
    ring_across = [(c * spots + a, (1 - c) * spots + b) for c in range(2) for a, b in ring]

    outgoing = call(
        mask_kernel,
        out_shape=shape((members, rows_dev, 2 * BLK), BF16),
        in_specs=[pl.BlockSpec(memory_space=pltpu.SMEM), vmem],
        out_specs=vmem,
    )(block_mask, adjacency)
    received = lax.all_to_all(outgoing, group, split_axis=0, concat_axis=0, tiled=True)
    pieces = call(pieces_kernel, out_shape=shape((4, rows_dev, inner), BF16))(outgoing)
    by_ring = lax.ppermute(pieces[2], ("z1", "z0", "zhi"), ring)
    across = lax.ppermute(pieces[3], ("core", "z1", "z0", "zhi"), ring_across)
    by_ring, swapped = lax.optimization_barrier((by_ring, pieces[1]))
    direct = [pieces[0], other_core(swapped), by_ring, across]
    block, shard, row_sum = call(
        form_kernel,
        grid=(nx,),
        in_specs=[pl.BlockSpec((2 * ny, rows_dev, 2 * BLK), lambda i: (i, 0, 0))]
        + [pl.BlockSpec((rows_dev, width), lambda i: (0, i))] * 4,
        out_specs=[
            pl.BlockSpec((4, rows_dev, width), lambda i: (0, 0, i)),
            pl.BlockSpec((4 * part, width), lambda i: (0, i)),
            pl.BlockSpec((1, 4 * rows_dev), lambda i: (0, 0)),
        ],
        out_shape=[
            shape((4, rows_dev, inner), BF16),
            shape((4 * part, inner), BF16),
            shape((1, 4 * rows_dev), F32),
        ],
        scratch_shapes=[
            pltpu.VMEM((4, rows_dev, BLK), F32),
            pltpu.VMEM((4, rows_dev, BLK), F32),
        ],
    )(received, *direct)
    near = jnp.concatenate([shard, lax.ppermute(shard, "z0", SWAP)], axis=0)
    def step_x(piece, d):
        return lax.ppermute(piece, "x", [(i, (i + d) % nx) for i in range(nx)])

    partial = row_sum.reshape(1, 2, 2, 1, 1, rows_dev).transpose(0, 2, 1, 3, 4, 5)
    partial = jnp.broadcast_to(partial, (nx, 2, 2, 2, ny, rows_dev))
    partial = lax.all_to_all(
        partial.reshape(2 * members * 2, rows_dev),
        ("x", "core", "z1", "z0", "y"),
        split_axis=0,
        concat_axis=0,
        tiled=True,
    )
    partial = jnp.sum(partial.reshape(nx, 2, 2, 2, ny, rows_dev), axis=1)
    degree = jnp.where(
        z1 == 0,
        partial[:, 0] + partial[:, 1, ::-1],
        partial[:, 1] + partial[:, 0, ::-1],
    ).reshape(1, inner)
    rows = [near] + [
        lax.ppermute(near, "y", [(i, (i + d) % ny) for i in range(ny)]) for d in range(1, ny)
    ]

    own_block = block.reshape(2 * BLK, inner)
    blocks = [own_block, step_x(own_block, 1)]
    if nx == 4:
        after = step_x(own_block, -1)
        before = blocks[1]
        blocks = [own_block, before, step_x(before[:BLK], 1), step_x(after[BLK:], -1), after]
    tile_cols = nx * BLK

    def product(group):
        return call(
            functools.partial(product_kernel, group, ny),
            in_specs=[vmem] * (ny + len(blocks) + 1),
            out_specs=[vmem] * 2,
            out_shape=[shape((nc, part, tile_cols), t) for t in (F32, BF16)],
            scratch_shapes=[pltpu.VMEM((ny * near.shape[0], inner), BF16), pltpu.VMEM((tile_cols, inner), BF16)],
        )(*rows, *blocks, degree)

    mine, theirs = product(1)
    sent = (mine + other_core(theirs).astype(F32)).astype(BF16)
    got = lax.all_to_all(
        jnp.stack([sent, sent]),
        ("z1", "z0"),
        split_axis=0,
        concat_axis=0,
        tiled=True,
        axis_index_groups=[[0, 3], [1, 2]],
    )
    got = lax.dynamic_index_in_dim(got, 1 - z1, 0, keepdims=False)
    mine, theirs = product(0)
    summed = mine + other_core(theirs).astype(F32) + got.astype(F32)
    prune = prune_mask.reshape(nc, nx, nc, nx)
    prune = lax.dynamic_index_in_dim(prune, x_id, 1, keepdims=False)
    prune = lax.dynamic_index_in_dim(prune, c_id, 1, keepdims=False)
    prune = jnp.repeat(prune.astype(F32), BLK, axis=1)
    pruned = summed * summed * prune[:, None, :]
    mass = lax.psum(jnp.sum(pruned, axis=(0, 1)), "core")
    mass = jnp.sum(spread(mass.reshape(-1, BLK), ("x", "zhi"), nx * nl), axis=0).reshape(-1)
    return pruned * (node_count / mass)[None, None, :]


def solution(mesh):
    rows, cols, layers = mesh.devices.shape
    devices = mesh.devices.reshape(rows // 2, 2, 2, 2, cols // 4, layers)
    split = Mesh(devices, AXES)
    in_specs = (P(("z1", "z0", "y"), ("x", "core"), None), P(), P())
    out_specs = P(None, ("x", "core", "zhi"), ("z1", "z0", "y"))
    return jax.shard_map(
        on_device, mesh=split, in_specs=in_specs, out_specs=out_specs, check_vma=False
    )
```

```python
import functools

import jax
import jax.numpy as jnp
from jax import lax
from jax.experimental import pallas as pl
from jax.experimental.pallas import tpu as pltpu
from jax.sharding import Mesh, PartitionSpec as P

BLK = 128
INTERPRET = False
BF16, F32 = jnp.bfloat16, jnp.float32
PARAMS = dict(vmem_limit_bytes=48 * 1024 * 1024)
AXES = ("x", "core", "z1", "z0", "y", "zhi")
SWAP = [(0, 1), (1, 0)]


def where_am_i():
    return tuple(lax.axis_index(a) for a in AXES)


def mask_kernel(mask_ref, adj_ref, out_ref):
    x_id, _, z1, z0, y_id, _ = where_am_i()
    nx, ny = lax.axis_size("x"), lax.axis_size("y")
    row = ((z1 * 2 + z0) * ny + y_id) * nx + x_id
    for x in range(nx):
        for z in range(4):
            low, high = (z, 0) if z < 2 else (3 - z, 1)
            base = (x * 2 + jnp.where(z1 == 0, low, 1 - low)) * ny
            for y in range(ny):
                block = (z * ny + y) * nx + x
                keep = mask_ref[row, block].astype(F32).astype(BF16)
                out_ref[base + y, :, high * BLK : (high + 1) * BLK] = (
                    adj_ref[0, :, block * BLK : (block + 1) * BLK] * keep
                )


def pieces_kernel(flip, out_ref, piece_ref):
    core, z1 = lax.axis_index("core"), lax.axis_index("z1")
    nx, ny = lax.axis_size("x"), lax.axis_size("y")
    n = out_ref.shape[1]
    low_lanes = lax.broadcasted_iota(jnp.int32, (n, BLK), 1) < n
    lanes = pl.ds(pl.multiple_of((z1 + flip) % 2 * BLK, BLK), BLK)
    for p in range(nx * ny):
        x, z0, q = p // ny, p % ny // (ny // 2), p % (ny // 2)
        spot = (x * 2 + (z0 ^ flip)) * ny + 2 * q
        a = out_ref[spot, :, lanes].astype(F32)
        b = out_ref[spot + 1, :, lanes].astype(F32)
        cols = slice(p * BLK, (p + 1) * BLK)
        first = jnp.where(low_lanes, a, pltpu.roll(b, n, 1))
        second = jnp.where(low_lanes, pltpu.roll(a, n, 1), b)
        piece_ref[core, :, cols] = first.astype(BF16)
        piece_ref[1 - core, :, cols] = second.astype(BF16)


def form_kernel(
    recv_ref, d00, d01, d10, d11, block_ref, shard_ref, sum_ref, flip_ref, acc_ref
):
    x_id, core, z1, z0, y_id, l_id = where_am_i()
    ny, nl = lax.axis_size("y"), lax.axis_size("zhi")
    n = d00.shape[0]
    part = n // nl
    step = pl.program_id(0)
    own_source = z0 * ny + y_id
    own_p = jnp.where(step == x_id, own_source // 2, -1)
    r = lax.broadcasted_iota(jnp.int32, (n, BLK), 0)
    k = lax.broadcasted_iota(jnp.int32, (n, BLK), 1)
    diagonal = jnp.where(k == r + own_source % 2 * n, 1.0, 0.0)

    @pl.when(step == 0)
    def _():
        acc_ref[...] = jnp.zeros_like(acc_ref)

    for p in range(ny):
        cols = slice(p * BLK, (p + 1) * BLK)
        got = recv_ref[2 * p : 2 * p + 2].reshape(BLK, 2 * BLK).astype(F32)
        flip_ref[...] = got.T.reshape(flip_ref.shape)
        for i, direct in enumerate((d00, d01, d10, d11)):
            b, c = i // 2, i % 2
            spot = jnp.where(z1 == b, 0, 2) + jnp.where(core == c, 0, 1)
            value = direct[:, cols].astype(F32) + flip_ref[spot]
            if i == 0:
                value = value + jnp.where(own_p == p, diagonal, 0.0)
            rounded = value.astype(BF16)
            block_ref[2 * jnp.where(core == c, 0, 1) + b, :, cols] = rounded
            acc_ref[spot] += rounded.astype(F32)

    rows = pl.ds(pl.multiple_of(l_id * part, part), part)
    for group in range(4):
        spot = group % 2 * 2 + (group // 2 ^ z1)
        shard_ref[group * part : (group + 1) * part, :] = block_ref[spot, rows, :]

    @pl.when(step == pl.num_programs(0) - 1)
    def _():
        sums = jnp.sum(acc_ref[...].reshape(4 * n, BLK).T, axis=0, keepdims=True)
        for group in range(4):
            spot = group % 2 * 2 + group // 2
            sum_ref[spot : spot + 1, :] = sums[:, group * n : (group + 1) * n]


def product_kernel(group, ny, *refs):
    left_refs, refs = refs[:ny], refs[ny:]
    *right_refs, degree_ref, mine_ref, theirs_ref, left, right = refs
    if len(right_refs) == 5:
        own_ref, before_ref, far0_ref, far1_ref, after_ref = right_refs
        right_refs = [(own_ref,) * 2, (before_ref,) * 2, (far0_ref, far1_ref), (after_ref,) * 2]
    else:
        right_refs = [(ref,) * 2 for ref in right_refs]
    x_id, core, z1, z0, y_id, _ = where_am_i()
    nx = lax.axis_size("x")
    lines = left_refs[0].shape[0]
    part = lines // 8
    for i, ref in enumerate(left_refs):
        left[i * lines : (i + 1) * lines, :] = ref[...]
    inverse = 1.0 / degree_ref[...]
    n = BLK // 2
    for d, pair in enumerate(right_refs):
        for core_rows, ref in enumerate(pair):
            low = (2 * core_rows if ref.shape[0] > BLK else 0) * n + group * n
            block = ref[low : low + n, :].astype(F32)
            rows = slice(d * BLK + core_rows * n, d * BLK + (core_rows + 1) * n)
            right[rows, :] = (block * inverse).astype(BF16)
    value = lax.dot_general(
        left[...], right[...], (((1,), (1,)), ((), ())), preferred_element_type=F32
    )
    value = value.reshape(8 * ny, part, right.shape[0])
    for sel in range(2):
        low = jnp.where((z0 + z1) % 2 == sel, 0, 1)
        for y in range(ny):
            for b in range(2):
                c = jnp.where(b == 0, low, 3 - low) * ny + (y_id - y + ny) % ny
                spot = ((y * 2 + sel) * 2 + b) * 2
                first, second = value[spot], value[spot + 1]
                mine = jnp.where(core == 0, first, second)
                theirs = jnp.where(core == 0, second, first).astype(BF16)
                for e in range(nx):
                    x = (x_id - e + nx) % nx
                    lanes = pl.ds(pl.multiple_of(x * BLK, BLK), BLK)
                    mine_ref[c, :, lanes] = mine[:, e * BLK : (e + 1) * BLK]
                    theirs_ref[c, :, lanes] = theirs[:, e * BLK : (e + 1) * BLK]


def on_device(adjacency, block_mask, prune_mask):
    rows_dev = adjacency.shape[1]
    node_count = adjacency.shape[2]
    nx, nk, _, _, ny, nl = (lax.axis_size(a) for a in AXES)
    nc = 4 * ny
    x_id, k_id, z1, z0, y_id, _ = where_am_i()
    c_id = (z1 * 2 + z0) * ny + y_id
    part = rows_dev // nl
    inner = node_count // 4
    width = inner // nx
    shape = jax.ShapeDtypeStruct
    vmem = pl.BlockSpec(memory_space=pltpu.VMEM)
    params = pltpu.CompilerParams(**PARAMS)
    call = functools.partial(pl.pallas_call, compiler_params=params, interpret=INTERPRET)
    group = ("x", "z0", "y")
    members = nx * 2 * ny

    def other_core(value):
        return lax.ppermute(value, "core", SWAP)

    def spread(piece, axes, count):
        wide = jnp.broadcast_to(piece[None], (count,) + piece.shape)
        return lax.all_to_all(wide, axes, split_axis=0, concat_axis=0, tiled=True)

    ring = []
    for l in range(nl):
        ring += [(0 * nl + l, 3 * nl + (l - 1) % nl), (3 * nl + l, 0 * nl + (l + 1) % nl)]
        ring += [(1 * nl + l, 2 * nl + l), (2 * nl + l, 1 * nl + l)]
    spots = 4 * nl
    ring_across = [(c * spots + a, (1 - c) * spots + b) for c in range(2) for a, b in ring]

    outgoing = call(
        mask_kernel,
        out_shape=shape((members, rows_dev, 2 * BLK), BF16),
        in_specs=[pl.BlockSpec(memory_space=pltpu.SMEM), vmem],
        out_specs=vmem,
    )(block_mask, adjacency)
    received = lax.all_to_all(outgoing, group, split_axis=0, concat_axis=0, tiled=True)
    ring_pieces, core_pieces = (
        call(
            functools.partial(pieces_kernel, flip), out_shape=shape((2, rows_dev, inner), BF16)
        )(outgoing)
        for flip in (1, 0)
    )
    by_ring = lax.ppermute(ring_pieces[0], ("z1", "z0", "zhi"), ring)
    across = lax.ppermute(ring_pieces[1], ("core", "z1", "z0", "zhi"), ring_across)
    by_ring, swapped = lax.optimization_barrier((by_ring, core_pieces[1]))
    direct = [core_pieces[0], other_core(swapped), by_ring, across]
    block, shard, row_sum = call(
        form_kernel,
        grid=(nx,),
        in_specs=[pl.BlockSpec((2 * ny, rows_dev, 2 * BLK), lambda i: (i, 0, 0))]
        + [pl.BlockSpec((rows_dev, width), lambda i: (0, i))] * 4,
        out_specs=[
            pl.BlockSpec((4, rows_dev, width), lambda i: (0, 0, i)),
            pl.BlockSpec((4 * part, width), lambda i: (0, i)),
            pl.BlockSpec((4, rows_dev), lambda i: (0, 0)),
        ],
        out_shape=[
            shape((4, rows_dev, inner), BF16),
            shape((4 * part, inner), BF16),
            shape((4, rows_dev), F32),
        ],
        scratch_shapes=[
            pltpu.VMEM((4, rows_dev, BLK), F32),
            pltpu.VMEM((4, rows_dev, BLK), F32),
        ],
    )(received, *direct)
    near = jnp.concatenate([shard, lax.ppermute(shard, "z0", SWAP)], axis=0)
    def step_x(piece, d):
        return lax.ppermute(piece, "x", [(i, (i + d) % nx) for i in range(nx)])

    partial = row_sum.reshape(1, 2, 2, 1, 1, rows_dev)
    partial = jnp.broadcast_to(partial, (nx, 2, 2, 2, ny, rows_dev))
    partial = lax.all_to_all(
        partial.reshape(2 * members * 2, rows_dev),
        ("x", "core", "z1", "z0", "y"),
        split_axis=0,
        concat_axis=0,
        tiled=True,
    )
    partial = jnp.sum(partial.reshape(nx, 2, 2, 2, ny, rows_dev), axis=1)
    degree = jnp.where(
        z1 == 0,
        partial[:, 0] + partial[:, 1, ::-1],
        partial[:, 1] + partial[:, 0, ::-1],
    ).reshape(1, inner)
    rows = [near] + [
        lax.ppermute(near, "y", [(i, (i + d) % ny) for i in range(ny)]) for d in range(1, ny)
    ]

    own_block = block.reshape(2 * BLK, inner)
    blocks = [own_block, step_x(own_block, 1)]
    if nx == 4:
        after = step_x(own_block, -1)
        before = blocks[1]
        blocks = [own_block, before, step_x(before[:BLK], 1), step_x(after[BLK:], -1), after]
    tile_cols = nx * BLK

    def product(group):
        return call(
            functools.partial(product_kernel, group, ny),
            in_specs=[vmem] * (ny + len(blocks) + 1),
            out_specs=[vmem] * 2,
            out_shape=[shape((nc, part, tile_cols), t) for t in (F32, BF16)],
            scratch_shapes=[pltpu.VMEM((ny * near.shape[0], inner), BF16), pltpu.VMEM((tile_cols, inner), BF16)],
        )(*rows, *blocks, degree)

    mine, theirs = product(1)
    sent = (mine + other_core(theirs).astype(F32)).astype(BF16)
    got = lax.all_to_all(
        jnp.stack([sent, sent]),
        ("z1", "z0"),
        split_axis=0,
        concat_axis=0,
        tiled=True,
        axis_index_groups=[[0, 3], [1, 2]],
    )
    got = lax.dynamic_index_in_dim(got, 1 - z1, 0, keepdims=False)
    mine, theirs = product(0)
    summed = mine + other_core(theirs).astype(F32) + got.astype(F32)
    prune = prune_mask.reshape(nc, nx, nc, nx)
    prune = lax.dynamic_index_in_dim(prune, x_id, 1, keepdims=False)
    prune = lax.dynamic_index_in_dim(prune, c_id, 1, keepdims=False)
    prune = jnp.repeat(prune.astype(F32), BLK, axis=1)
    pruned = lax.optimization_barrier(summed * summed * prune[:, None, :])
    mass = lax.psum(jnp.sum(pruned, axis=(0, 1)), "core")
    mass = jnp.sum(spread(mass.reshape(-1, BLK), ("x", "zhi"), nx * nl), axis=0).reshape(-1)
    return pruned * (node_count / mass)[None, None, :]


def solution(mesh):
    rows, cols, layers = mesh.devices.shape
    devices = mesh.devices.reshape(rows // 2, 2, 2, 2, cols // 4, layers)
    split = Mesh(devices, AXES)
    in_specs = (P(("z1", "z0", "y"), ("x", "core"), None), P(), P())
    out_specs = P(None, ("x", "core", "zhi"), ("z1", "z0", "y"))
    return jax.shard_map(
        on_device, mesh=split, in_specs=in_specs, out_specs=out_specs, check_vma=False
    )
```

```python
import functools

import jax
import jax.numpy as jnp
from jax import lax
from jax.experimental import pallas as pl
from jax.experimental.pallas import tpu as pltpu
from jax.sharding import Mesh, PartitionSpec as P

BLK = 128
INTERPRET = False
BF16, F32 = jnp.bfloat16, jnp.float32
PARAMS = dict(vmem_limit_bytes=48 * 1024 * 1024)
AXES = ("x", "core", "z1", "z0", "y", "zhi")
SWAP = [(0, 1), (1, 0)]


def where_am_i():
    return tuple(lax.axis_index(a) for a in AXES)


def mask_kernel(mask_ref, adj_ref, out_ref):
    x_id, _, z1, z0, y_id, _ = where_am_i()
    nx, ny = lax.axis_size("x"), lax.axis_size("y")
    row = ((z1 * 2 + z0) * ny + y_id) * nx + x_id
    for x in range(nx):
        for z in range(4):
            low, high = (z, 0) if z < 2 else (3 - z, 1)
            base = (x * 2 + jnp.where(z1 == 0, low, 1 - low)) * ny
            for y in range(ny):
                block = (z * ny + y) * nx + x
                keep = mask_ref[row, block].astype(F32).astype(BF16)
                out_ref[base + y, :, high * BLK : (high + 1) * BLK] = (
                    adj_ref[0, :, block * BLK : (block + 1) * BLK] * keep
                )


def pieces_kernel(flip, out_ref, piece_ref):
    core, z1 = lax.axis_index("core"), lax.axis_index("z1")
    nx, ny = lax.axis_size("x"), lax.axis_size("y")
    n = out_ref.shape[1]
    low_lanes = lax.broadcasted_iota(jnp.int32, (n, BLK), 1) < n
    lanes = pl.ds(pl.multiple_of((z1 + flip) % 2 * BLK, BLK), BLK)
    for p in range(nx * ny):
        x, z0, q = p // ny, p % ny // (ny // 2), p % (ny // 2)
        spot = (x * 2 + (z0 ^ flip)) * ny + 2 * q
        a = out_ref[spot, :, lanes].astype(F32)
        b = out_ref[spot + 1, :, lanes].astype(F32)
        cols = slice(p * BLK, (p + 1) * BLK)
        first = jnp.where(low_lanes, a, pltpu.roll(b, n, 1))
        second = jnp.where(low_lanes, pltpu.roll(a, n, 1), b)
        piece_ref[core, :, cols] = first.astype(BF16)
        piece_ref[1 - core, :, cols] = second.astype(BF16)


def form_kernel(
    recv_ref, d00, d01, d10, d11, block_ref, shard_ref, sum_ref, flip_ref, acc_ref
):
    x_id, core, z1, z0, y_id, l_id = where_am_i()
    ny, nl = lax.axis_size("y"), lax.axis_size("zhi")
    n = d00.shape[0]
    part = n // nl
    step = pl.program_id(0)
    own_source = z0 * ny + y_id
    own_p = jnp.where(step == x_id, own_source // 2, -1)
    r = lax.broadcasted_iota(jnp.int32, (n, BLK), 0)
    k = lax.broadcasted_iota(jnp.int32, (n, BLK), 1)
    diagonal = jnp.where(k == r + own_source % 2 * n, 1.0, 0.0)

    @pl.when(step == 0)
    def _():
        acc_ref[...] = jnp.zeros_like(acc_ref)

    for p in range(ny):
        cols = slice(p * BLK, (p + 1) * BLK)
        got = recv_ref[2 * p : 2 * p + 2].reshape(BLK, 2 * BLK).astype(F32)
        flip_ref[...] = got.T.reshape(flip_ref.shape)
        for i, direct in enumerate((d00, d01, d10, d11)):
            b, c = i // 2, i % 2
            spot = jnp.where(z1 == b, 0, 2) + jnp.where(core == c, 0, 1)
            value = direct[:, cols].astype(F32) + flip_ref[spot]
            if i == 0:
                value = value + jnp.where(own_p == p, diagonal, 0.0)
            rounded = value.astype(BF16)
            block_ref[2 * jnp.where(core == c, 0, 1) + b, :, cols] = rounded
            acc_ref[spot] += rounded.astype(F32)

    rows = pl.ds(pl.multiple_of(l_id * part, part), part)
    for group in range(4):
        spot = group % 2 * 2 + (group // 2 ^ z1)
        shard_ref[group * part : (group + 1) * part, :] = block_ref[spot, rows, :]

    @pl.when(step == pl.num_programs(0) - 1)
    def _():
        sums = jnp.sum(acc_ref[...].reshape(4 * n, BLK).T, axis=0, keepdims=True)
        for group in range(4):
            spot = group % 2 * 2 + group // 2
            sum_ref[spot : spot + 1, :] = sums[:, group * n : (group + 1) * n]


def product_kernel(group, ny, *refs):
    left_refs, refs = refs[:ny], refs[ny:]
    *right_refs, degree_ref, mine_ref, theirs_ref, left, right = refs
    if len(right_refs) == 5:
        own_ref, before_ref, far0_ref, far1_ref, after_ref = right_refs
        right_refs = [(own_ref,) * 2, (before_ref,) * 2, (far0_ref, far1_ref), (after_ref,) * 2]
    else:
        right_refs = [(ref,) * 2 for ref in right_refs]
    x_id, core, z1, z0, y_id, _ = where_am_i()
    nx = lax.axis_size("x")
    lines = left_refs[0].shape[0]
    part = lines // 8
    for i, ref in enumerate(left_refs):
        left[i * lines : (i + 1) * lines, :] = ref[...]
    inverse = 1.0 / degree_ref[...]
    n = BLK // 2
    for d, pair in enumerate(right_refs):
        for core_rows, ref in enumerate(pair):
            low = (2 * core_rows if ref.shape[0] > BLK else 0) * n + group * n
            block = ref[low : low + n, :].astype(F32)
            rows = slice(d * BLK + core_rows * n, d * BLK + (core_rows + 1) * n)
            right[rows, :] = (block * inverse).astype(BF16)
    value = lax.dot_general(
        left[...], right[...], (((1,), (1,)), ((), ())), preferred_element_type=F32
    )
    value = value.reshape(8 * ny, part, right.shape[0])
    for sel in range(2):
        low = jnp.where((z0 + z1) % 2 == sel, 0, 1)
        for y in range(ny):
            for b in range(2):
                c = jnp.where(b == 0, low, 3 - low) * ny + (y_id - y + ny) % ny
                spot = ((y * 2 + sel) * 2 + b) * 2
                first, second = value[spot], value[spot + 1]
                mine = jnp.where(core == 0, first, second)
                theirs = jnp.where(core == 0, second, first).astype(BF16)
                for e in range(nx):
                    x = (x_id - e + nx) % nx
                    lanes = pl.ds(pl.multiple_of(x * BLK, BLK), BLK)
                    mine_ref[c, :, lanes] = mine[:, e * BLK : (e + 1) * BLK]
                    theirs_ref[c, :, lanes] = theirs[:, e * BLK : (e + 1) * BLK]


def on_device(adjacency, block_mask, prune_mask):
    rows_dev = adjacency.shape[1]
    node_count = adjacency.shape[2]
    nx, nk, _, _, ny, nl = (lax.axis_size(a) for a in AXES)
    nc = 4 * ny
    x_id, k_id, z1, z0, y_id, _ = where_am_i()
    c_id = (z1 * 2 + z0) * ny + y_id
    part = rows_dev // nl
    inner = node_count // 4
    width = inner // nx
    shape = jax.ShapeDtypeStruct
    vmem = pl.BlockSpec(memory_space=pltpu.VMEM)
    params = pltpu.CompilerParams(**PARAMS)
    call = functools.partial(pl.pallas_call, compiler_params=params, interpret=INTERPRET)
    group = ("x", "z0", "y")
    members = nx * 2 * ny

    def other_core(value):
        return lax.ppermute(value, "core", SWAP)

    def spread(piece, axes, count):
        wide = jnp.broadcast_to(piece[None], (count,) + piece.shape)
        return lax.all_to_all(wide, axes, split_axis=0, concat_axis=0, tiled=True)

    ring = []
    for l in range(nl):
        ring += [(0 * nl + l, 3 * nl + (l - 1) % nl), (3 * nl + l, 0 * nl + (l + 1) % nl)]
        ring += [(1 * nl + l, 2 * nl + l), (2 * nl + l, 1 * nl + l)]
    spots = 4 * nl
    ring_across = [(c * spots + a, (1 - c) * spots + b) for c in range(2) for a, b in ring]

    outgoing = call(
        mask_kernel,
        out_shape=shape((members, rows_dev, 2 * BLK), BF16),
        in_specs=[pl.BlockSpec(memory_space=pltpu.SMEM), vmem],
        out_specs=vmem,
    )(block_mask, adjacency)
    received = lax.all_to_all(outgoing, group, split_axis=0, concat_axis=0, tiled=True)
    ring_pieces, core_pieces = (
        call(
            functools.partial(pieces_kernel, flip), out_shape=shape((2, rows_dev, inner), BF16)
        )(outgoing)
        for flip in (1, 0)
    )
    by_ring = lax.ppermute(ring_pieces[0], ("z1", "z0", "zhi"), ring)
    across = lax.ppermute(ring_pieces[1], ("core", "z1", "z0", "zhi"), ring_across)
    by_ring, swapped = lax.optimization_barrier((by_ring, core_pieces[1]))
    direct = [core_pieces[0], other_core(swapped), by_ring, across]
    block, shard, row_sum = call(
        form_kernel,
        grid=(nx,),
        in_specs=[pl.BlockSpec((2 * ny, rows_dev, 2 * BLK), lambda i: (i, 0, 0))]
        + [pl.BlockSpec((rows_dev, width), lambda i: (0, i))] * 4,
        out_specs=[
            pl.BlockSpec((4, rows_dev, width), lambda i: (0, 0, i)),
            pl.BlockSpec((4 * part, width), lambda i: (0, i)),
            pl.BlockSpec((4, rows_dev), lambda i: (0, 0)),
        ],
        out_shape=[
            shape((4, rows_dev, inner), BF16),
            shape((4 * part, inner), BF16),
            shape((4, rows_dev), F32),
        ],
        scratch_shapes=[
            pltpu.VMEM((4, rows_dev, BLK), F32),
            pltpu.VMEM((4, rows_dev, BLK), F32),
        ],
    )(received, *direct)
    near = jnp.concatenate([shard, lax.ppermute(shard, "z0", SWAP)], axis=0)
    def step_x(piece, d):
        return lax.ppermute(piece, "x", [(i, (i + d) % nx) for i in range(nx)])

    partial = row_sum.reshape(1, 2, 2, 1, 1, rows_dev)
    partial = jnp.broadcast_to(partial, (nx, 2, 2, 2, ny, rows_dev))
    partial = lax.all_to_all(
        partial.reshape(2 * members * 2, rows_dev),
        ("x", "core", "z1", "z0", "y"),
        split_axis=0,
        concat_axis=0,
        tiled=True,
    )
    partial = jnp.sum(partial.reshape(nx, 2, 2, 2, ny, rows_dev), axis=1)
    degree = jnp.where(
        z1 == 0,
        partial[:, 0] + partial[:, 1, ::-1],
        partial[:, 1] + partial[:, 0, ::-1],
    ).reshape(1, inner)
    rows = [near] + [
        lax.ppermute(near, "y", [(i, (i + d) % ny) for i in range(ny)]) for d in range(1, ny)
    ]

    own_block = block.reshape(2 * BLK, inner)
    blocks = [own_block, step_x(own_block, 1)]
    if nx == 4:
        after = step_x(own_block, -1)
        before = blocks[1]
        blocks = [own_block, before, step_x(before[:BLK], 1), step_x(after[BLK:], -1), after]
    tile_cols = nx * BLK

    def product(group):
        return call(
            functools.partial(product_kernel, group, ny),
            in_specs=[vmem] * (ny + len(blocks) + 1),
            out_specs=[vmem] * 2,
            out_shape=[shape((nc, part, tile_cols), t) for t in (F32, BF16)],
            scratch_shapes=[pltpu.VMEM((ny * near.shape[0], inner), BF16), pltpu.VMEM((tile_cols, inner), BF16)],
        )(*rows, *blocks, degree)

    mine, theirs = product(1)
    sent = (mine + other_core(theirs).astype(F32)).astype(BF16)
    got = lax.all_to_all(
        jnp.stack([sent, sent]),
        ("z1", "z0"),
        split_axis=0,
        concat_axis=0,
        tiled=True,
        axis_index_groups=[[0, 3], [1, 2]],
    )
    got = lax.dynamic_index_in_dim(got, 1 - z1, 0, keepdims=False)
    mine, theirs = product(0)
    summed = mine + other_core(theirs).astype(F32) + got.astype(F32)
    prune = prune_mask.reshape(nc, nx, nc, nx)
    prune = lax.dynamic_index_in_dim(prune, x_id, 1, keepdims=False)
    prune = lax.dynamic_index_in_dim(prune, c_id, 1, keepdims=False)
    prune = jnp.repeat(prune.astype(F32), BLK, axis=1)
    pruned = lax.optimization_barrier(summed * summed * prune[:, None, :])
    mass = jnp.sum(pruned, axis=(0, 1)).reshape(-1, BLK)
    mass = jnp.sum(spread(mass, ("x", "core", "zhi"), nx * nk * nl), axis=0).reshape(-1)
    return pruned * (node_count / mass)[None, None, :]


def solution(mesh):
    rows, cols, layers = mesh.devices.shape
    devices = mesh.devices.reshape(rows // 2, 2, 2, 2, cols // 4, layers)
    split = Mesh(devices, AXES)
    in_specs = (P(("z1", "z0", "y"), ("x", "core"), None), P(), P())
    out_specs = P(None, ("x", "core", "zhi"), ("z1", "z0", "y"))
    return jax.shard_map(
        on_device, mesh=split, in_specs=in_specs, out_specs=out_specs, check_vma=False
    )
```

```python
import functools

import jax
import jax.numpy as jnp
from jax import lax
from jax.experimental import pallas as pl
from jax.experimental.pallas import tpu as pltpu
from jax.sharding import Mesh, PartitionSpec as P

BLK = 128
INTERPRET = False
BF16, F32 = jnp.bfloat16, jnp.float32
PARAMS = dict(vmem_limit_bytes=48 * 1024 * 1024)
AXES = ("x", "core", "z1", "z0", "y", "zhi")
SWAP = [(0, 1), (1, 0)]


def where_am_i():
    return tuple(lax.axis_index(a) for a in AXES)


def mask_kernel(mask_ref, adj_ref, out_ref):
    x_id, _, z1, z0, y_id, _ = where_am_i()
    nx, ny = lax.axis_size("x"), lax.axis_size("y")
    row = ((z1 * 2 + z0) * ny + y_id) * nx + x_id
    for x in range(nx):
        for z in range(4):
            low, high = (z, 0) if z < 2 else (3 - z, 1)
            base = (x * 2 + jnp.where(z1 == 0, low, 1 - low)) * ny
            for y in range(ny):
                block = (z * ny + y) * nx + x
                keep = mask_ref[row, block].astype(F32).astype(BF16)
                out_ref[base + y, :, high * BLK : (high + 1) * BLK] = (
                    adj_ref[0, :, block * BLK : (block + 1) * BLK] * keep
                )


def pieces_kernel(flip, out_ref, piece_ref):
    core, z1 = lax.axis_index("core"), lax.axis_index("z1")
    nx, ny = lax.axis_size("x"), lax.axis_size("y")
    n = out_ref.shape[1]
    low_lanes = lax.broadcasted_iota(jnp.int32, (n, BLK), 1) < n
    lanes = pl.ds(pl.multiple_of((z1 + flip) % 2 * BLK, BLK), BLK)
    for p in range(nx * ny):
        x, z0, q = p // ny, p % ny // (ny // 2), p % (ny // 2)
        spot = (x * 2 + (z0 ^ flip)) * ny + 2 * q
        a = out_ref[spot, :, lanes].astype(F32)
        b = out_ref[spot + 1, :, lanes].astype(F32)
        cols = slice(p * BLK, (p + 1) * BLK)
        first = jnp.where(low_lanes, a, pltpu.roll(b, n, 1))
        second = jnp.where(low_lanes, pltpu.roll(a, n, 1), b)
        piece_ref[core, :, cols] = first.astype(BF16)
        piece_ref[1 - core, :, cols] = second.astype(BF16)


def form_kernel(
    recv_ref, d00, d01, d10, d11, block_ref, shard_ref, sum_ref, flip_ref, acc_ref
):
    x_id, core, z1, z0, y_id, l_id = where_am_i()
    ny, nl = lax.axis_size("y"), lax.axis_size("zhi")
    n = d00.shape[0]
    part = n // nl
    step = pl.program_id(0)
    own_source = z0 * ny + y_id
    own_p = jnp.where(step == x_id, own_source // 2, -1)
    r = lax.broadcasted_iota(jnp.int32, (n, BLK), 0)
    k = lax.broadcasted_iota(jnp.int32, (n, BLK), 1)
    diagonal = jnp.where(k == r + own_source % 2 * n, 1.0, 0.0)

    @pl.when(step == 0)
    def _():
        acc_ref[...] = jnp.zeros_like(acc_ref)

    for p in range(ny):
        cols = slice(p * BLK, (p + 1) * BLK)
        got = recv_ref[2 * p : 2 * p + 2].reshape(BLK, 2 * BLK).astype(F32)
        flip_ref[...] = got.T.reshape(flip_ref.shape)
        for i, direct in enumerate((d00, d01, d10, d11)):
            b, c = i // 2, i % 2
            spot = jnp.where(z1 == b, 0, 2) + jnp.where(core == c, 0, 1)
            value = direct[:, cols].astype(F32) + flip_ref[spot]
            if i == 0:
                value = value + jnp.where(own_p == p, diagonal, 0.0)
            rounded = value.astype(BF16)
            block_ref[2 * jnp.where(core == c, 0, 1) + b, :, cols] = rounded
            acc_ref[spot] += rounded.astype(F32)

    rows = pl.ds(pl.multiple_of(l_id * part, part), part)
    for group in range(4):
        spot = group % 2 * 2 + (group // 2 ^ z1)
        shard_ref[group * part : (group + 1) * part, :] = block_ref[spot, rows, :]

    @pl.when(step == pl.num_programs(0) - 1)
    def _():
        sums = jnp.sum(acc_ref[...].reshape(4 * n, BLK).T, axis=0, keepdims=True)
        for group in range(4):
            spot = group % 2 * 2 + group // 2
            sum_ref[spot : spot + 1, :] = sums[:, group * n : (group + 1) * n]


def product_kernel(group, ny, *refs):
    left_refs, refs = refs[:ny], refs[ny:]
    *right_refs, degree_ref, mine_ref, theirs_ref, left, right = refs
    if len(right_refs) == 5:
        own_ref, before_ref, far0_ref, far1_ref, after_ref = right_refs
        right_refs = [(own_ref,) * 2, (before_ref,) * 2, (far0_ref, far1_ref), (after_ref,) * 2]
    else:
        right_refs = [(ref,) * 2 for ref in right_refs]
    x_id, core, z1, z0, y_id, _ = where_am_i()
    nx = lax.axis_size("x")
    lines = left_refs[0].shape[0]
    part = lines // 8
    for i, ref in enumerate(left_refs):
        left[i * lines : (i + 1) * lines, :] = ref[...]
    inverse = 1.0 / degree_ref[...]
    n = BLK // 2
    for d, pair in enumerate(right_refs):
        for core_rows, ref in enumerate(pair):
            low = (2 * core_rows if ref.shape[0] > BLK else 0) * n + group * n
            block = ref[low : low + n, :].astype(F32)
            rows = slice(d * BLK + core_rows * n, d * BLK + (core_rows + 1) * n)
            right[rows, :] = (block * inverse).astype(BF16)
    value = lax.dot_general(
        left[...], right[...], (((1,), (1,)), ((), ())), preferred_element_type=F32
    )
    value = value.reshape(8 * ny, part, right.shape[0])
    for sel in range(2):
        low = jnp.where((z0 + z1) % 2 == sel, 0, 1)
        for y in range(ny):
            for b in range(2):
                c = jnp.where(b == 0, low, 3 - low) * ny + (y_id - y + ny) % ny
                spot = ((y * 2 + sel) * 2 + b) * 2
                first, second = value[spot], value[spot + 1]
                mine = jnp.where(core == 0, first, second)
                theirs = jnp.where(core == 0, second, first).astype(BF16)
                for e in range(nx):
                    x = (x_id - e + nx) % nx
                    lanes = pl.ds(pl.multiple_of(x * BLK, BLK), BLK)
                    mine_ref[c, :, lanes] = mine[:, e * BLK : (e + 1) * BLK]
                    theirs_ref[c, :, lanes] = theirs[:, e * BLK : (e + 1) * BLK]


def on_device(adjacency, block_mask, prune_mask):
    rows_dev = adjacency.shape[1]
    node_count = adjacency.shape[2]
    nx, nk, _, _, ny, nl = (lax.axis_size(a) for a in AXES)
    nc = 4 * ny
    x_id, k_id, z1, z0, y_id, _ = where_am_i()
    c_id = (z1 * 2 + z0) * ny + y_id
    part = rows_dev // nl
    inner = node_count // 4
    width = inner // nx
    shape = jax.ShapeDtypeStruct
    vmem = pl.BlockSpec(memory_space=pltpu.VMEM)
    params = pltpu.CompilerParams(**PARAMS)
    call = functools.partial(pl.pallas_call, compiler_params=params, interpret=INTERPRET)
    group = ("x", "z0", "y")
    members = nx * 2 * ny

    def other_core(value):
        return lax.ppermute(value, "core", SWAP)

    def spread(piece, axes, count):
        wide = jnp.broadcast_to(piece[None], (count,) + piece.shape)
        return lax.all_to_all(wide, axes, split_axis=0, concat_axis=0, tiled=True)

    ring = []
    for l in range(nl):
        ring += [(0 * nl + l, 3 * nl + (l - 1) % nl), (3 * nl + l, 0 * nl + (l + 1) % nl)]
        ring += [(1 * nl + l, 2 * nl + l), (2 * nl + l, 1 * nl + l)]
    spots = 4 * nl
    ring_across = [(c * spots + a, (1 - c) * spots + b) for c in range(2) for a, b in ring]

    outgoing = call(
        mask_kernel,
        out_shape=shape((members, rows_dev, 2 * BLK), BF16),
        in_specs=[pl.BlockSpec(memory_space=pltpu.SMEM), vmem],
        out_specs=vmem,
    )(block_mask, adjacency)
    received = lax.all_to_all(outgoing, group, split_axis=0, concat_axis=0, tiled=True)
    ring_pieces, core_pieces = (
        call(
            functools.partial(pieces_kernel, flip), out_shape=shape((2, rows_dev, inner), BF16)
        )(outgoing)
        for flip in (1, 0)
    )
    by_ring = lax.ppermute(ring_pieces[0], ("z1", "z0", "zhi"), ring)
    across = lax.ppermute(ring_pieces[1], ("core", "z1", "z0", "zhi"), ring_across)
    by_ring, swapped = lax.optimization_barrier((by_ring, core_pieces[1]))
    direct = [core_pieces[0], other_core(swapped), by_ring, across]
    block, shard, row_sum = call(
        form_kernel,
        grid=(nx,),
        in_specs=[pl.BlockSpec((2 * ny, rows_dev, 2 * BLK), lambda i: (i, 0, 0))]
        + [pl.BlockSpec((rows_dev, width), lambda i: (0, i))] * 4,
        out_specs=[
            pl.BlockSpec((4, rows_dev, width), lambda i: (0, 0, i)),
            pl.BlockSpec((4 * part, width), lambda i: (0, i)),
            pl.BlockSpec((4, rows_dev), lambda i: (0, 0)),
        ],
        out_shape=[
            shape((4, rows_dev, inner), BF16),
            shape((4 * part, inner), BF16),
            shape((4, rows_dev), F32),
        ],
        scratch_shapes=[
            pltpu.VMEM((4, rows_dev, BLK), F32),
            pltpu.VMEM((4, rows_dev, BLK), F32),
        ],
    )(received, *direct)
    near = jnp.concatenate([shard, lax.ppermute(shard, "z0", SWAP)], axis=0)
    def step_x(piece, d):
        return lax.ppermute(piece, "x", [(i, (i + d) % nx) for i in range(nx)])

    partial = jnp.broadcast_to(row_sum.reshape(2, 2, 1, 1, rows_dev), (2, 2, 2, ny, rows_dev))
    partial = lax.all_to_all(
        partial.reshape(8 * ny, rows_dev),
        ("core", "z1", "z0", "y"),
        split_axis=0,
        concat_axis=0,
        tiled=True,
    )
    rows = [near] + [
        lax.ppermute(near, "y", [(i, (i + d) % ny) for i in range(ny)]) for d in range(1, ny)
    ]

    own_block = block.reshape(2 * BLK, inner)
    blocks = [own_block, step_x(own_block, 1)]
    if nx == 4:
        after = step_x(own_block, -1)
        before, after, partial = lax.optimization_barrier((blocks[1], after, partial))
        blocks = [own_block, before, step_x(before[:BLK], 1), step_x(after[BLK:], -1), after]

    partial = jnp.sum(partial.reshape(2, 2, 2, ny, rows_dev), axis=0)
    degree = jnp.where(
        z1 == 0, partial[0] + partial[1, ::-1], partial[1] + partial[0, ::-1]
    )
    degree = spread(degree.reshape(-1, BLK), "x", nx).reshape(1, inner)

    tile_cols = nx * BLK

    def product(group):
        return call(
            functools.partial(product_kernel, group, ny),
            in_specs=[vmem] * (ny + len(blocks) + 1),
            out_specs=[vmem] * 2,
            out_shape=[shape((nc, part, tile_cols), t) for t in (F32, BF16)],
            scratch_shapes=[pltpu.VMEM((ny * near.shape[0], inner), BF16), pltpu.VMEM((tile_cols, inner), BF16)],
        )(*rows, *blocks, degree)

    mine, theirs = product(1)
    sent = (mine + other_core(theirs).astype(F32)).astype(BF16)
    got = lax.all_to_all(
        jnp.stack([sent, sent]),
        ("z1", "z0"),
        split_axis=0,
        concat_axis=0,
        tiled=True,
        axis_index_groups=[[0, 3], [1, 2]],
    )
    got = lax.dynamic_index_in_dim(got, 1 - z1, 0, keepdims=False)
    mine, theirs = product(0)
    summed = mine + other_core(theirs).astype(F32) + got.astype(F32)
    prune = prune_mask.reshape(nc, nx, nc, nx)
    prune = lax.dynamic_index_in_dim(prune, x_id, 1, keepdims=False)
    prune = lax.dynamic_index_in_dim(prune, c_id, 1, keepdims=False)
    prune = jnp.repeat(prune.astype(F32), BLK, axis=1)
    pruned = lax.optimization_barrier(summed * summed * prune[:, None, :])
    mass = jnp.sum(pruned, axis=(0, 1)).reshape(-1, BLK)
    mass = jnp.sum(spread(mass, ("x", "core", "zhi"), nx * nk * nl), axis=0).reshape(-1)
    return pruned * (node_count / mass)[None, None, :]


def solution(mesh):
    rows, cols, layers = mesh.devices.shape
    devices = mesh.devices.reshape(rows // 2, 2, 2, 2, cols // 4, layers)
    split = Mesh(devices, AXES)
    in_specs = (P(("z1", "z0", "y"), ("x", "core"), None), P(), P())
    out_specs = P(None, ("x", "core", "zhi"), ("z1", "z0", "y"))
    return jax.shard_map(
        on_device, mesh=split, in_specs=in_specs, out_specs=out_specs, check_vma=False
    )
```

```python
import functools

import jax
import jax.numpy as jnp
from jax import lax
from jax.experimental import pallas as pl
from jax.experimental.pallas import tpu as pltpu
from jax.sharding import Mesh, PartitionSpec as P

BLK = 128
INTERPRET = False
BF16, F32 = jnp.bfloat16, jnp.float32
PARAMS = dict(vmem_limit_bytes=48 * 1024 * 1024)
AXES = ("x", "core", "z1", "z0", "y", "zhi")
SWAP = [(0, 1), (1, 0)]


def where_am_i():
    return tuple(lax.axis_index(a) for a in AXES)


def mask_kernel(mask_ref, adj_ref, out_ref):
    x_id, _, z1, z0, y_id, _ = where_am_i()
    nx, ny = lax.axis_size("x"), lax.axis_size("y")
    row = ((z1 * 2 + z0) * ny + y_id) * nx + x_id
    for x in range(nx):
        for z in range(4):
            low, high = (z, 0) if z < 2 else (3 - z, 1)
            base = (x * 2 + jnp.where(z1 == 0, low, 1 - low)) * ny
            for y in range(ny):
                block = (z * ny + y) * nx + x
                keep = mask_ref[row, block].astype(F32).astype(BF16)
                out_ref[base + y, :, high * BLK : (high + 1) * BLK] = (
                    adj_ref[0, :, block * BLK : (block + 1) * BLK] * keep
                )


def pieces_kernel(flip, out_ref, piece_ref):
    core, z1 = lax.axis_index("core"), lax.axis_index("z1")
    nx, ny = lax.axis_size("x"), lax.axis_size("y")
    n = out_ref.shape[1]
    low_lanes = lax.broadcasted_iota(jnp.int32, (n, BLK), 1) < n
    lanes = pl.ds(pl.multiple_of((z1 + flip) % 2 * BLK, BLK), BLK)
    for p in range(nx * ny):
        x, z0, q = p // ny, p % ny // (ny // 2), p % (ny // 2)
        spot = (x * 2 + (z0 ^ flip)) * ny + 2 * q
        a = out_ref[spot, :, lanes].astype(F32)
        b = out_ref[spot + 1, :, lanes].astype(F32)
        cols = slice(p * BLK, (p + 1) * BLK)
        first = jnp.where(low_lanes, a, pltpu.roll(b, n, 1))
        second = jnp.where(low_lanes, pltpu.roll(a, n, 1), b)
        piece_ref[core, :, cols] = first.astype(BF16)
        piece_ref[1 - core, :, cols] = second.astype(BF16)


def form_kernel(
    recv_ref, d00, d01, d10, d11, block_ref, shard_ref, sum_ref, flip_ref, acc_ref
):
    x_id, core, z1, z0, y_id, l_id = where_am_i()
    ny, nl = lax.axis_size("y"), lax.axis_size("zhi")
    n = d00.shape[0]
    part = n // nl
    step = pl.program_id(0)
    own_source = z0 * ny + y_id
    own_p = jnp.where(step == x_id, own_source // 2, -1)
    r = lax.broadcasted_iota(jnp.int32, (n, BLK), 0)
    k = lax.broadcasted_iota(jnp.int32, (n, BLK), 1)
    diagonal = jnp.where(k == r + own_source % 2 * n, 1.0, 0.0)

    @pl.when(step == 0)
    def _():
        acc_ref[...] = jnp.zeros_like(acc_ref)

    for p in range(ny):
        cols = slice(p * BLK, (p + 1) * BLK)
        got = recv_ref[2 * p : 2 * p + 2].reshape(BLK, 2 * BLK)
        flip_ref[...] = got.T.astype(F32).reshape(flip_ref.shape)
        for i, direct in enumerate((d00, d01, d10, d11)):
            b, c = i // 2, i % 2
            spot = jnp.where(z1 == b, 0, 2) + jnp.where(core == c, 0, 1)
            value = direct[:, cols].astype(F32) + flip_ref[spot]
            if i == 0:
                value = value + jnp.where(own_p == p, diagonal, 0.0)
            rounded = value.astype(BF16)
            block_ref[2 * jnp.where(core == c, 0, 1) + b, :, cols] = rounded
            acc_ref[spot] += rounded.astype(F32)

    rows = pl.ds(pl.multiple_of(l_id * part, part), part)
    for group in range(4):
        spot = group % 2 * 2 + (group // 2 ^ z1)
        shard_ref[group * part : (group + 1) * part, :] = block_ref[spot, rows, :]

    @pl.when(step == pl.num_programs(0) - 1)
    def _():
        sums = jnp.sum(acc_ref[...].reshape(4 * n, BLK).T, axis=0, keepdims=True)
        for group in range(4):
            spot = group % 2 * 2 + group // 2
            sum_ref[spot : spot + 1, :] = sums[:, group * n : (group + 1) * n]


def product_kernel(group, ny, *refs):
    left_refs, refs = refs[:ny], refs[ny:]
    *right_refs, degree_ref, mine_ref, theirs_ref, left, right = refs
    if len(right_refs) == 5:
        own_ref, before_ref, far0_ref, far1_ref, after_ref = right_refs
        right_refs = [(own_ref,) * 2, (before_ref,) * 2, (far0_ref, far1_ref), (after_ref,) * 2]
    else:
        right_refs = [(ref,) * 2 for ref in right_refs]
    x_id, core, z1, z0, y_id, _ = where_am_i()
    nx = lax.axis_size("x")
    lines = left_refs[0].shape[0]
    part = lines // 8
    for i, ref in enumerate(left_refs):
        left[i * lines : (i + 1) * lines, :] = ref[...]
    inverse = 1.0 / degree_ref[...]
    n = BLK // 2
    for d, pair in enumerate(right_refs):
        for core_rows, ref in enumerate(pair):
            low = (2 * core_rows if ref.shape[0] > BLK else 0) * n + group * n
            block = ref[low : low + n, :].astype(F32)
            rows = slice(d * BLK + core_rows * n, d * BLK + (core_rows + 1) * n)
            right[rows, :] = (block * inverse).astype(BF16)
    value = lax.dot_general(
        left[...], right[...], (((1,), (1,)), ((), ())), preferred_element_type=F32
    )
    value = value.reshape(8 * ny, part, right.shape[0])
    for sel in range(2):
        low = jnp.where((z0 + z1) % 2 == sel, 0, 1)
        for y in range(ny):
            for b in range(2):
                c = jnp.where(b == 0, low, 3 - low) * ny + (y_id - y + ny) % ny
                spot = ((y * 2 + sel) * 2 + b) * 2
                first, second = value[spot], value[spot + 1]
                mine = jnp.where(core == 0, first, second)
                theirs = jnp.where(core == 0, second, first).astype(BF16)
                for e in range(nx):
                    x = (x_id - e + nx) % nx
                    lanes = pl.ds(pl.multiple_of(x * BLK, BLK), BLK)
                    mine_ref[c, :, lanes] = mine[:, e * BLK : (e + 1) * BLK]
                    theirs_ref[c, :, lanes] = theirs[:, e * BLK : (e + 1) * BLK]


def on_device(adjacency, block_mask, prune_mask):
    rows_dev = adjacency.shape[1]
    node_count = adjacency.shape[2]
    nx, nk, _, _, ny, nl = (lax.axis_size(a) for a in AXES)
    nc = 4 * ny
    x_id, k_id, z1, z0, y_id, _ = where_am_i()
    c_id = (z1 * 2 + z0) * ny + y_id
    part = rows_dev // nl
    inner = node_count // 4
    width = inner // nx
    shape = jax.ShapeDtypeStruct
    vmem = pl.BlockSpec(memory_space=pltpu.VMEM)
    params = pltpu.CompilerParams(**PARAMS)
    call = functools.partial(pl.pallas_call, compiler_params=params, interpret=INTERPRET)
    group = ("x", "z0", "y")
    members = nx * 2 * ny

    def other_core(value):
        return lax.ppermute(value, "core", SWAP)

    def spread(piece, axes, count):
        wide = jnp.broadcast_to(piece[None], (count,) + piece.shape)
        return lax.all_to_all(wide, axes, split_axis=0, concat_axis=0, tiled=True)

    ring = []
    for l in range(nl):
        ring += [(0 * nl + l, 3 * nl + (l - 1) % nl), (3 * nl + l, 0 * nl + (l + 1) % nl)]
        ring += [(1 * nl + l, 2 * nl + l), (2 * nl + l, 1 * nl + l)]
    spots = 4 * nl
    ring_across = [(c * spots + a, (1 - c) * spots + b) for c in range(2) for a, b in ring]

    outgoing = call(
        mask_kernel,
        out_shape=shape((members, rows_dev, 2 * BLK), BF16),
        in_specs=[pl.BlockSpec(memory_space=pltpu.SMEM), vmem],
        out_specs=vmem,
    )(block_mask, adjacency)
    received = lax.all_to_all(outgoing, group, split_axis=0, concat_axis=0, tiled=True)
    ring_pieces, core_pieces = (
        call(
            functools.partial(pieces_kernel, flip), out_shape=shape((2, rows_dev, inner), BF16)
        )(outgoing)
        for flip in (1, 0)
    )
    by_ring = lax.ppermute(ring_pieces[0], ("z1", "z0", "zhi"), ring)
    across = lax.ppermute(ring_pieces[1], ("core", "z1", "z0", "zhi"), ring_across)
    by_ring, swapped = lax.optimization_barrier((by_ring, core_pieces[1]))
    direct = [core_pieces[0], other_core(swapped), by_ring, across]
    block, shard, row_sum = call(
        form_kernel,
        grid=(nx,),
        in_specs=[pl.BlockSpec((2 * ny, rows_dev, 2 * BLK), lambda i: (i, 0, 0))]
        + [pl.BlockSpec((rows_dev, width), lambda i: (0, i))] * 4,
        out_specs=[
            pl.BlockSpec((4, rows_dev, width), lambda i: (0, 0, i)),
            pl.BlockSpec((4 * part, width), lambda i: (0, i)),
            pl.BlockSpec((4, rows_dev), lambda i: (0, 0)),
        ],
        out_shape=[
            shape((4, rows_dev, inner), BF16),
            shape((4 * part, inner), BF16),
            shape((4, rows_dev), F32),
        ],
        scratch_shapes=[
            pltpu.VMEM((4, rows_dev, BLK), F32),
            pltpu.VMEM((4, rows_dev, BLK), F32),
        ],
    )(received, *direct)
    near = jnp.concatenate([shard, lax.ppermute(shard, "z0", SWAP)], axis=0)
    def step_x(piece, d):
        return lax.ppermute(piece, "x", [(i, (i + d) % nx) for i in range(nx)])

    partial = jnp.broadcast_to(row_sum.reshape(2, 2, 1, 1, rows_dev), (2, 2, 2, ny, rows_dev))
    partial = lax.all_to_all(
        partial.reshape(8 * ny, rows_dev),
        ("core", "z1", "z0", "y"),
        split_axis=0,
        concat_axis=0,
        tiled=True,
    )
    rows = [near] + [
        lax.ppermute(near, "y", [(i, (i + d) % ny) for i in range(ny)]) for d in range(1, ny)
    ]

    own_block = block.reshape(2 * BLK, inner)
    blocks = [own_block, step_x(own_block, 1)]
    if nx == 4:
        after = step_x(own_block, -1)
        before, after, partial = lax.optimization_barrier((blocks[1], after, partial))
        blocks = [own_block, before, step_x(before[:BLK], 1), step_x(after[BLK:], -1), after]

    partial = jnp.sum(partial.reshape(2, 2, 2, ny, rows_dev), axis=0)
    degree = jnp.where(
        z1 == 0, partial[0] + partial[1, ::-1], partial[1] + partial[0, ::-1]
    )
    degree = spread(degree.reshape(-1, BLK), "x", nx).reshape(1, inner)

    tile_cols = nx * BLK

    def product(group):
        return call(
            functools.partial(product_kernel, group, ny),
            in_specs=[vmem] * (ny + len(blocks) + 1),
            out_specs=[vmem] * 2,
            out_shape=[shape((nc, part, tile_cols), t) for t in (F32, BF16)],
            scratch_shapes=[pltpu.VMEM((ny * near.shape[0], inner), BF16), pltpu.VMEM((tile_cols, inner), BF16)],
        )(*rows, *blocks, degree)

    mine, theirs = product(1)
    sent = (mine + other_core(theirs).astype(F32)).astype(BF16)
    got = lax.all_to_all(
        jnp.stack([sent, sent]),
        ("z1", "z0"),
        split_axis=0,
        concat_axis=0,
        tiled=True,
        axis_index_groups=[[0, 3], [1, 2]],
    )
    got = lax.dynamic_index_in_dim(got, 1 - z1, 0, keepdims=False)
    mine, theirs = product(0)
    summed = mine + other_core(theirs).astype(F32) + got.astype(F32)
    prune = prune_mask.reshape(nc, nx, nc, nx)
    prune = lax.dynamic_index_in_dim(prune, x_id, 1, keepdims=False)
    prune = lax.dynamic_index_in_dim(prune, c_id, 1, keepdims=False)
    prune = jnp.repeat(prune.astype(F32), BLK, axis=1)
    pruned = lax.optimization_barrier(summed * summed * prune[:, None, :])
    mass = jnp.sum(pruned, axis=(0, 1)).reshape(-1, BLK)
    mass = jnp.sum(spread(mass, ("x", "core", "zhi"), nx * nk * nl), axis=0).reshape(-1)
    return pruned * (node_count / mass)[None, None, :]


def solution(mesh):
    rows, cols, layers = mesh.devices.shape
    devices = mesh.devices.reshape(rows // 2, 2, 2, 2, cols // 4, layers)
    split = Mesh(devices, AXES)
    in_specs = (P(("z1", "z0", "y"), ("x", "core"), None), P(), P())
    out_specs = P(None, ("x", "core", "zhi"), ("z1", "z0", "y"))
    return jax.shard_map(
        on_device, mesh=split, in_specs=in_specs, out_specs=out_specs, check_vma=False
    )
```

```python
import functools

import jax
import jax.numpy as jnp
from jax import lax
from jax.experimental import pallas as pl
from jax.experimental.pallas import tpu as pltpu
from jax.sharding import Mesh, PartitionSpec as P

BLK = 128
INTERPRET = False
BF16, F32 = jnp.bfloat16, jnp.float32
PARAMS = dict(vmem_limit_bytes=48 * 1024 * 1024)
AXES = ("x", "core", "z1", "z0", "y", "zhi")
SWAP = [(0, 1), (1, 0)]


def where_am_i():
    return tuple(lax.axis_index(a) for a in AXES)


def mask_kernel(mask_ref, adj_ref, out_ref):
    x_id, _, z1, z0, y_id, _ = where_am_i()
    nx, ny = lax.axis_size("x"), lax.axis_size("y")
    row = ((z1 * 2 + z0) * ny + y_id) * nx + x_id
    for x in range(nx):
        for z in range(4):
            low, high = (z, 0) if z < 2 else (3 - z, 1)
            base = (x * 2 + jnp.where(z1 == 0, low, 1 - low)) * ny
            for y in range(ny):
                block = (z * ny + y) * nx + x
                tile = adj_ref[0, :, block * BLK : (block + 1) * BLK]
                out_ref[base + y, :, high * BLK : (high + 1) * BLK] = jnp.where(
                    mask_ref[row, block] != 0, tile, jnp.zeros_like(tile)
                )


def pieces_kernel(flip, out_ref, piece_ref):
    core, z1 = lax.axis_index("core"), lax.axis_index("z1")
    nx, ny = lax.axis_size("x"), lax.axis_size("y")
    n = out_ref.shape[1]
    low_lanes = lax.broadcasted_iota(jnp.int32, (n, BLK), 1) < n
    lanes = pl.ds(pl.multiple_of((z1 + flip) % 2 * BLK, BLK), BLK)
    for p in range(nx * ny):
        x, z0, q = p // ny, p % ny // (ny // 2), p % (ny // 2)
        spot = (x * 2 + (z0 ^ flip)) * ny + 2 * q
        a = out_ref[spot, :, lanes].astype(F32)
        b = out_ref[spot + 1, :, lanes].astype(F32)
        cols = slice(p * BLK, (p + 1) * BLK)
        first = jnp.where(low_lanes, a, pltpu.roll(b, n, 1))
        second = jnp.where(low_lanes, pltpu.roll(a, n, 1), b)
        piece_ref[core, :, cols] = first.astype(BF16)
        piece_ref[1 - core, :, cols] = second.astype(BF16)


def form_kernel(
    recv_ref, d00, d01, d10, d11, block_ref, shard_ref, sum_ref, flip_ref, acc_ref
):
    x_id, core, z1, z0, y_id, l_id = where_am_i()
    ny, nl = lax.axis_size("y"), lax.axis_size("zhi")
    n = d00.shape[0]
    part = n // nl
    step = pl.program_id(0)
    own_source = z0 * ny + y_id
    own_p = jnp.where(step == x_id, own_source // 2, -1)
    r = lax.broadcasted_iota(jnp.int32, (n, BLK), 0)
    k = lax.broadcasted_iota(jnp.int32, (n, BLK), 1)
    diagonal = jnp.where(k == r + own_source % 2 * n, 1.0, 0.0)

    @pl.when(step == 0)
    def _():
        acc_ref[...] = jnp.zeros_like(acc_ref)

    for p in range(ny):
        cols = slice(p * BLK, (p + 1) * BLK)
        got = recv_ref[2 * p : 2 * p + 2].reshape(BLK, 2 * BLK)
        flip_ref[...] = got.T.astype(F32).reshape(flip_ref.shape)
        for i, direct in enumerate((d00, d01, d10, d11)):
            b, c = i // 2, i % 2
            spot = jnp.where(z1 == b, 0, 2) + jnp.where(core == c, 0, 1)
            value = direct[:, cols].astype(F32) + flip_ref[spot]
            if i == 0:
                value = value + jnp.where(own_p == p, diagonal, 0.0)
            rounded = value.astype(BF16)
            block_ref[2 * jnp.where(core == c, 0, 1) + b, :, cols] = rounded
            acc_ref[spot] += rounded.astype(F32)

    rows = pl.ds(pl.multiple_of(l_id * part, part), part)
    for group in range(4):
        spot = group % 2 * 2 + (group // 2 ^ z1)
        shard_ref[group * part : (group + 1) * part, :] = block_ref[spot, rows, :]

    @pl.when(step == pl.num_programs(0) - 1)
    def _():
        sums = jnp.sum(acc_ref[...].reshape(4 * n, BLK).T, axis=0, keepdims=True)
        for group in range(4):
            spot = group % 2 * 2 + group // 2
            sum_ref[spot : spot + 1, :] = sums[:, group * n : (group + 1) * n]


def product_kernel(group, ny, *refs):
    left_refs, refs = refs[:ny], refs[ny:]
    *right_refs, degree_ref, mine_ref, theirs_ref, left, right = refs
    if len(right_refs) == 5:
        own_ref, before_ref, far0_ref, far1_ref, after_ref = right_refs
        right_refs = [(own_ref,) * 2, (before_ref,) * 2, (far0_ref, far1_ref), (after_ref,) * 2]
    else:
        right_refs = [(ref,) * 2 for ref in right_refs]
    x_id, core, z1, z0, y_id, _ = where_am_i()
    nx = lax.axis_size("x")
    lines = left_refs[0].shape[0]
    part = lines // 8
    for i, ref in enumerate(left_refs):
        left[i * lines : (i + 1) * lines, :] = ref[...]
    inverse = 1.0 / degree_ref[...]
    n = BLK // 2
    for d, pair in enumerate(right_refs):
        for core_rows, ref in enumerate(pair):
            low = (2 * core_rows if ref.shape[0] > BLK else 0) * n + group * n
            block = ref[low : low + n, :].astype(F32)
            rows = slice(d * BLK + core_rows * n, d * BLK + (core_rows + 1) * n)
            right[rows, :] = (block * inverse).astype(BF16)
    value = lax.dot_general(
        left[...], right[...], (((1,), (1,)), ((), ())), preferred_element_type=F32
    )
    value = value.reshape(8 * ny, part, right.shape[0])
    for sel in range(2):
        low = jnp.where((z0 + z1) % 2 == sel, 0, 1)
        for y in range(ny):
            for b in range(2):
                c = jnp.where(b == 0, low, 3 - low) * ny + (y_id - y + ny) % ny
                spot = ((y * 2 + sel) * 2 + b) * 2
                first, second = value[spot], value[spot + 1]
                mine = jnp.where(core == 0, first, second)
                theirs = jnp.where(core == 0, second, first).astype(BF16)
                for e in range(nx):
                    x = (x_id - e + nx) % nx
                    lanes = pl.ds(pl.multiple_of(x * BLK, BLK), BLK)
                    mine_ref[c, :, lanes] = mine[:, e * BLK : (e + 1) * BLK]
                    theirs_ref[c, :, lanes] = theirs[:, e * BLK : (e + 1) * BLK]


def on_device(adjacency, block_mask, prune_mask):
    rows_dev = adjacency.shape[1]
    node_count = adjacency.shape[2]
    nx, nk, _, _, ny, nl = (lax.axis_size(a) for a in AXES)
    nc = 4 * ny
    x_id, k_id, z1, z0, y_id, _ = where_am_i()
    c_id = (z1 * 2 + z0) * ny + y_id
    part = rows_dev // nl
    inner = node_count // 4
    width = inner // nx
    shape = jax.ShapeDtypeStruct
    vmem = pl.BlockSpec(memory_space=pltpu.VMEM)
    params = pltpu.CompilerParams(**PARAMS)
    call = functools.partial(pl.pallas_call, compiler_params=params, interpret=INTERPRET)
    group = ("x", "z0", "y")
    members = nx * 2 * ny

    def other_core(value):
        return lax.ppermute(value, "core", SWAP)

    def spread(piece, axes, count):
        wide = jnp.broadcast_to(piece[None], (count,) + piece.shape)
        return lax.all_to_all(wide, axes, split_axis=0, concat_axis=0, tiled=True)

    ring = []
    for l in range(nl):
        ring += [(0 * nl + l, 3 * nl + (l - 1) % nl), (3 * nl + l, 0 * nl + (l + 1) % nl)]
        ring += [(1 * nl + l, 2 * nl + l), (2 * nl + l, 1 * nl + l)]
    spots = 4 * nl
    ring_across = [(c * spots + a, (1 - c) * spots + b) for c in range(2) for a, b in ring]

    outgoing = call(
        mask_kernel,
        out_shape=shape((members, rows_dev, 2 * BLK), BF16),
        in_specs=[pl.BlockSpec(memory_space=pltpu.SMEM), vmem],
        out_specs=vmem,
    )(block_mask, adjacency)
    received = lax.all_to_all(outgoing, group, split_axis=0, concat_axis=0, tiled=True)
    ring_pieces, core_pieces = (
        call(
            functools.partial(pieces_kernel, flip), out_shape=shape((2, rows_dev, inner), BF16)
        )(outgoing)
        for flip in (1, 0)
    )
    by_ring = lax.ppermute(ring_pieces[0], ("z1", "z0", "zhi"), ring)
    across = lax.ppermute(ring_pieces[1], ("core", "z1", "z0", "zhi"), ring_across)
    by_ring, swapped = lax.optimization_barrier((by_ring, core_pieces[1]))
    direct = [core_pieces[0], other_core(swapped), by_ring, across]
    block, shard, row_sum = call(
        form_kernel,
        grid=(nx,),
        in_specs=[pl.BlockSpec((2 * ny, rows_dev, 2 * BLK), lambda i: (i, 0, 0))]
        + [pl.BlockSpec((rows_dev, width), lambda i: (0, i))] * 4,
        out_specs=[
            pl.BlockSpec((4, rows_dev, width), lambda i: (0, 0, i)),
            pl.BlockSpec((4 * part, width), lambda i: (0, i)),
            pl.BlockSpec((4, rows_dev), lambda i: (0, 0)),
        ],
        out_shape=[
            shape((4, rows_dev, inner), BF16),
            shape((4 * part, inner), BF16),
            shape((4, rows_dev), F32),
        ],
        scratch_shapes=[
            pltpu.VMEM((4, rows_dev, BLK), F32),
            pltpu.VMEM((4, rows_dev, BLK), F32),
        ],
    )(received, *direct)
    near = jnp.concatenate([shard, lax.ppermute(shard, "z0", SWAP)], axis=0)
    def step_x(piece, d):
        return lax.ppermute(piece, "x", [(i, (i + d) % nx) for i in range(nx)])

    partial = jnp.broadcast_to(row_sum.reshape(2, 2, 1, 1, rows_dev), (2, 2, 2, ny, rows_dev))
    partial = lax.all_to_all(
        partial.reshape(8 * ny, rows_dev),
        ("core", "z1", "z0", "y"),
        split_axis=0,
        concat_axis=0,
        tiled=True,
    )
    rows = [near] + [
        lax.ppermute(near, "y", [(i, (i + d) % ny) for i in range(ny)]) for d in range(1, ny)
    ]

    own_block = block.reshape(2 * BLK, inner)
    blocks = [own_block, step_x(own_block, 1)]
    if nx == 4:
        after = step_x(own_block, -1)
        before, after, partial = lax.optimization_barrier((blocks[1], after, partial))
        blocks = [own_block, before, step_x(before[:BLK], 1), step_x(after[BLK:], -1), after]

    partial = jnp.sum(partial.reshape(2, 2, 2, ny, rows_dev), axis=0)
    degree = jnp.where(
        z1 == 0, partial[0] + partial[1, ::-1], partial[1] + partial[0, ::-1]
    )
    degree = spread(degree.reshape(-1, BLK), "x", nx).reshape(1, inner)

    tile_cols = nx * BLK

    def product(group):
        return call(
            functools.partial(product_kernel, group, ny),
            in_specs=[vmem] * (ny + len(blocks) + 1),
            out_specs=[vmem] * 2,
            out_shape=[shape((nc, part, tile_cols), t) for t in (F32, BF16)],
            scratch_shapes=[pltpu.VMEM((ny * near.shape[0], inner), BF16), pltpu.VMEM((tile_cols, inner), BF16)],
        )(*rows, *blocks, degree)

    mine, theirs = product(1)
    sent = (mine + other_core(theirs).astype(F32)).astype(BF16)
    got = lax.all_to_all(
        jnp.stack([sent, sent]),
        ("z1", "z0"),
        split_axis=0,
        concat_axis=0,
        tiled=True,
        axis_index_groups=[[0, 3], [1, 2]],
    )
    got = lax.dynamic_index_in_dim(got, 1 - z1, 0, keepdims=False)
    mine, theirs = product(0)
    summed = mine + other_core(theirs).astype(F32) + got.astype(F32)
    prune = prune_mask.reshape(nc, nx, nc, nx)
    prune = lax.dynamic_index_in_dim(prune, x_id, 1, keepdims=False)
    prune = lax.dynamic_index_in_dim(prune, c_id, 1, keepdims=False)
    prune = jnp.repeat(prune.astype(F32), BLK, axis=1)
    pruned = lax.optimization_barrier(summed * summed * prune[:, None, :])
    mass = jnp.sum(pruned, axis=(0, 1)).reshape(-1, BLK)
    mass = jnp.sum(spread(mass, ("x", "core", "zhi"), nx * nk * nl), axis=0).reshape(-1)
    return pruned * (node_count / mass)[None, None, :]


def solution(mesh):
    rows, cols, layers = mesh.devices.shape
    devices = mesh.devices.reshape(rows // 2, 2, 2, 2, cols // 4, layers)
    split = Mesh(devices, AXES)
    in_specs = (P(("z1", "z0", "y"), ("x", "core"), None), P(), P())
    out_specs = P(None, ("x", "core", "zhi"), ("z1", "z0", "y"))
    return jax.shard_map(
        on_device, mesh=split, in_specs=in_specs, out_specs=out_specs, check_vma=False
    )
```
